32 devices in a mesh: row: 4 (over y, x), col: 2 (over core), ctx: 4 (over z).
Axes of the slice: x: 2, y: 2, z: 4, core: 2. Of those that a mesh axis runs over, the one named last changes fastest.
Arguments:
- queries: bfloat16 [4096, 6144], P(('col', 'ctx'), 'row'), may hold values from -16 to 16
- keys: bfloat16 [4096, 6144], P(('col', 'ctx'), 'row'), may hold values from -16 to 16
- values: bfloat16 [4096, 6144], P(('col', 'ctx'), 'row'), may hold values from -6 to 6
- out_weight: bfloat16 [6144, 6144], P('col', 'row'), may hold values from -0.078125 to 0.078125
- cotangent: bfloat16 [4096, 6144], P(('col', 'ctx'), 'row'), may hold values from -0.125 to 0.125
- block_mask: int32 [8, 8], replicated, may hold values from 0 to 1, as said below
Outputs:
- mixed_out: bfloat16 [4096, 6144], P(('col', 'ctx'), 'row')
- grad_weight: bfloat16 [6144, 6144], P(('col', 'ctx'), 'row')
The draws below stay inside these ranges and needn't reach their ends.
Inputs may be any that keep to these rules, and one draw needn't show every extreme that they name: block_mask[i, i] is 1 for every block i, and block_mask[i, j] is 0 for j > i.
All inputs are finite; a program needn't handle non-finite values.
Results may differ from the reference program's by a relative error of at most 0.013.
Values may be sent and summed in bfloat16 or wider, within the bound.
No kernel may reach another device: no remote copies, remote signals or barrier semaphores. Data moves between devices by JAX's collectives and lax.ppermute only.
A program may use at most 128 MiB of HBM per device.

```python
import math
import jax
import jax.numpy as jnp
from jax import lax

D = 6144
H = 48
HD = 128
BLOCK = 512
SEQ = 4096
NBLK = 8


def drawn_pair(key):
    base_key = jax.random.fold_in(key, 7)
    query_key, keys_key = jax.random.split(base_key, 2)
    query_draw = jnp.clip(jax.random.normal(query_key, (SEQ, D), jnp.float32), -6.0, 6.0) * 1.6
    key_draw = jnp.clip(jax.random.normal(keys_key, (SEQ, D), jnp.float32), -6.0, 6.0) * 1.6
    return (query_draw, key_draw)


def draw_queries(key, part):
    return drawn_pair(key)[0].astype(jnp.bfloat16)


def draw_keys(key, part):
    return drawn_pair(key)[1].astype(jnp.bfloat16)


def draw_block_mask(key, part):
    random_bits = jax.random.randint(jax.random.fold_in(key, 11), (NBLK, NBLK), 0, 2, dtype=jnp.int32)
    row_index = jnp.arange(NBLK, dtype=jnp.int32)[:, None]
    column_index = jnp.arange(NBLK, dtype=jnp.int32)[None, :]
    ones_block = jnp.ones((NBLK, NBLK), jnp.int32)
    zero_block = jnp.zeros((NBLK, NBLK), jnp.int32)
    return jnp.where(column_index == row_index, ones_block, jnp.where(column_index < row_index, random_bits, zero_block)).astype(jnp.int32)


def block_scale(key, dims, pieces, low, high):
    gain = 1.0
    for axis_at, blocks in pieces:
        draws = jax.random.uniform(jax.random.fold_in(jax.random.fold_in(key, 6), axis_at), (blocks,), jnp.float32, low / len(pieces), high / len(pieces))
        gain = gain * jnp.repeat(jnp.exp(draws), dims[axis_at] // blocks).reshape((-1,) + (1,) * (len(dims) - 1 - axis_at))
    return gain


def scatter_about(key, shape, width, bound, cuts=(), kind=jnp.bfloat16):
    result = jax.random.normal(key, shape, jnp.float32) * width
    if len(cuts) > 0:
        result = block_scale(key, shape, cuts, -0.22, 0.18) * result
    return jnp.clip(result, min=-bound, max=bound).astype(kind)


def setup_inputs(seed: int = 0) -> dict:
    seeds = jax.random.split(jax.random.key(seed), 7)
    return {
        "queries": draw_queries(jax.random.fold_in(seeds[6], 71), 0),
        "keys": draw_keys(jax.random.fold_in(seeds[6], 71), 0),
        "values": scatter_about(seeds[2], (SEQ, D), 1.0, 6.0, ((0, 8), (1, 4))),
        "out_weight": scatter_about(seeds[3], (D, D), D ** -0.5, 0.078125, ((0, 2), (1, 4))),
        "cotangent": scatter_about(seeds[4], (SEQ, D), 0.02, 0.125, ((0, 8), (1, 4))),
        "block_mask": draw_block_mask(jax.random.fold_in(seeds[6], 71), 0),
    }


NEGATIVE_FILL = -1e+30

def attend_head(query_head, key_head, value_head, block_mask):
    score_scale = 1.0 / math.sqrt(HD)

    def query_block(block_index):
        query_rows = lax.dynamic_slice_in_dim(query_head, block_index * BLOCK, BLOCK, 0)
        scores = jnp.dot(query_rows, key_head.T, preferred_element_type=jnp.float32) * score_scale
        mask_row = lax.dynamic_index_in_dim(block_mask, block_index, 0, keepdims=False)
        allowed = jnp.repeat(mask_row, BLOCK, total_repeat_length=SEQ) == 1
        scores = jnp.where(allowed[None, :], scores, NEGATIVE_FILL)
        row_max = lax.optimization_barrier(jnp.max(scores, axis=1, keepdims=True))
        weights = jnp.where(allowed[None, :], jnp.exp(scores - row_max), 0.0)
        row_sum = lax.optimization_barrier(jnp.sum(weights, axis=1, keepdims=True))
        weighted = jnp.dot(weights.astype(jnp.bfloat16), value_head, preferred_element_type=jnp.float32)
        return (weighted / row_sum).astype(jnp.bfloat16)
    blocks_out = lax.map(query_block, jnp.arange(NBLK, dtype=jnp.int32))
    return blocks_out.reshape(SEQ, HD)

def reference(queries, keys, values, out_weight, cotangent, block_mask):

    def per_head(head_index):
        offset = head_index * HD
        query_head = lax.dynamic_slice_in_dim(queries, offset, HD, 1)
        key_head = lax.dynamic_slice_in_dim(keys, offset, HD, 1)
        value_head = lax.dynamic_slice_in_dim(values, offset, HD, 1)
        return attend_head(query_head, key_head, value_head, block_mask)
    heads_out = lax.map(per_head, jnp.arange(H, dtype=jnp.int32))
    attended = jnp.transpose(heads_out, (1, 0, 2)).reshape(SEQ, D)
    mixed_out = jnp.dot(attended, out_weight, preferred_element_type=jnp.float32).astype(jnp.bfloat16)
    grad_weight = jnp.dot(attended.T, cotangent, preferred_element_type=jnp.float32).astype(jnp.bfloat16)
    return (mixed_out, grad_weight)
```

```python
import functools
import math

import jax
import jax.numpy as jnp
from jax import lax
from jax.experimental import pallas as pl
from jax.experimental.pallas import tpu as pltpu
from jax.sharding import PartitionSpec as P

HD = 128
BLOCK = 512
NEGATIVE_FILL = -1e30
HALF = 3
LOG2E = math.log2(math.e)
MIB = 1 << 20
VMEM_MIB = 56
ANY = pl.BlockSpec(memory_space=pl.ANY)
SMEM = pl.BlockSpec(memory_space=pltpu.SMEM)


def attend_block(carried, query_heads, key_block, value_block, allowed, score_scale):
    run_max, run_sum, weighted = carried
    tok_rows, head_count, head_size = query_heads.shape
    key_heads = key_block.reshape(key_block.shape[0], head_count, head_size)
    value_heads = value_block.reshape(value_block.shape[0], head_count, head_size)
    scores = (
        jnp.einsum("thd,uhd->thu", query_heads, key_heads, preferred_element_type=jnp.float32)
        * score_scale
    )
    scores = jnp.where(allowed[:, None, None], scores, NEGATIVE_FILL)
    new_max = jnp.maximum(run_max, jnp.max(scores, axis=2))
    correction = jnp.exp(run_max - new_max)
    weights = jnp.where(allowed[:, None, None], jnp.exp(scores - new_max[:, :, None]), 0.0)
    new_sum = run_sum * correction + jnp.sum(weights, axis=2)
    product = jnp.einsum(
        "thu,uhd->thd",
        weights.astype(jnp.bfloat16),
        value_heads,
        preferred_element_type=jnp.float32,
    )
    new_weighted = weighted * correction[:, :, None] + product
    return (new_max, new_sum, new_weighted)


def gathered_body(queries, keys, values, out_weight, cotangent, block_mask):
    tok_rows, feature_width = queries.shape
    head_count = feature_width // HD
    query_heads = queries.reshape(tok_rows, head_count, HD)
    score_scale = 1.0 / math.sqrt(HD)
    local_blocks = tok_rows // BLOCK
    first_block = lax.axis_index(("col", "ctx")) * local_blocks
    local_mask = lax.dynamic_slice_in_dim(block_mask, first_block, local_blocks, 0)
    start_state = (
        jnp.full((tok_rows, head_count), NEGATIVE_FILL, jnp.float32),
        jnp.zeros((tok_rows, head_count), jnp.float32),
        jnp.zeros((tok_rows, head_count, HD), jnp.float32),
    )
    key_piece = lax.all_gather(keys, ("col", "ctx"), axis=0, tiled=True)
    value_piece = lax.all_gather(values, ("col", "ctx"), axis=0, tiled=True)
    block_count = key_piece.shape[0] // BLOCK
    key_stack = key_piece.reshape(block_count, BLOCK, feature_width)
    value_stack = value_piece.reshape(block_count, BLOCK, feature_width)
    block_columns = jnp.arange(block_count, dtype=jnp.int32)

    def one_block(state_in, entries):
        key_block, value_block, block_column = entries
        mask_column = lax.dynamic_index_in_dim(local_mask, block_column, 1, keepdims=False)
        allowed = jnp.repeat(mask_column, BLOCK, total_repeat_length=tok_rows) == 1
        updated = attend_block(state_in, query_heads, key_block, value_block, allowed, score_scale)
        return (updated, None)

    state_out, _ = lax.scan(one_block, start_state, (key_stack, value_stack, block_columns))
    run_max, run_sum, weighted = state_out
    attended = (
        (weighted / run_sum[:, :, None]).reshape(tok_rows, feature_width).astype(jnp.bfloat16)
    )
    all_heads = lax.all_gather(attended, "row", axis=1, tiled=True)
    mixed_out = jnp.dot(
        all_heads,
        lax.all_gather(out_weight, "col", axis=0, tiled=True),
        preferred_element_type=jnp.float32,
    )
    grad_weight = lax.psum_scatter(
        lax.dot_general(
            all_heads, cotangent, (((0,), (0,)), ((), ())), preferred_element_type=jnp.float32
        ),
        ("col", "ctx"),
        scatter_dimension=0,
        tiled=True,
    )
    return (mixed_out.astype(jnp.bfloat16), grad_weight.astype(jnp.bfloat16))


def _params(mib):
    return pltpu.CompilerParams(vmem_limit_bytes=mib * MIB)


def _pack_kernel(place, *refs):
    columns, (send, keep) = refs[:6], refs[6:]
    for out, first in ((send, 0), (keep, 3)):
        out[0, 0] = columns[first][...]
        out[0, 1] = columns[first + 1][...]
        for n in range(BLOCK // HD):
            tile = slice(n * HD, (n + 1) * HD)
            out[0, 2, tile] = columns[first + 2][tile, :].T


def pack(head, place, q, k, v):
    shape = jax.ShapeDtypeStruct((2, 3, BLOCK, HD), jnp.bfloat16)

    def column(kept):
        def at(low, place_ref):
            side = place_ref[0] if kept else 1 - place_ref[0]
            return (0, 6 * low + 3 * side + head)

        return pl.BlockSpec((BLOCK, HD), at)

    out = pl.BlockSpec((1, 3, BLOCK, HD), lambda low, place_ref: (low, 0, 0, 0))
    return pl.pallas_call(
        _pack_kernel,
        grid_spec=pltpu.PrefetchScalarGridSpec(
            num_scalar_prefetch=1,
            grid=(2,),
            in_specs=[column(False)] * 3 + [column(True)] * 3,
            out_specs=(out, out),
        ),
        out_shape=(shape, shape),
        cost_estimate=pl.CostEstimate(flops=0, bytes_accessed=3 * MIB, transcendentals=0),
        name="pack",
    )(place, q, k, v, q, k, v)


def _attend_kernel(place, mask, *refs):
    own, other = refs[0], refs[1]
    out, out_t = refs[2:4]
    q_s, k_s, vt_s, sa_s, sb_s, m_s, l_s, acc_s, rows_s, cols_s, sems, other_sems = refs[4:]
    c, z = place[2], place[3]
    first = 4 * c
    copies = []
    others = []
    for s in range(4):
        b = s
        copies.append(pltpu.make_async_copy(own.at[s, 0], q_s.at[b], sems.at[2 * s]))
        copies.append(pltpu.make_async_copy(own.at[s, 1], k_s.at[first + b], sems.at[2 * s + 1]))
        for n in range(4):
            tile = pl.ds(n * HD, HD)
            copies.append(
                pltpu.make_async_copy(
                    own.at[s, 2, tile], vt_s.at[first + b, :, tile], sems.at[8 + 4 * s + n]
                )
            )
        others.append(pltpu.make_async_copy(other.at[s, 0], k_s.at[b], other_sems.at[s]))
        for n in range(4):
            tile = pl.ds(n * HD, HD)
            others.append(
                pltpu.make_async_copy(
                    other.at[s, 1, tile], vt_s.at[b, :, tile], other_sems.at[4 + 4 * s + n]
                )
            )
    for copy in copies:
        copy.start()

    @pl.when(c == 1)
    def _():
        for copy in others:
            copy.start()

    def listed(n, count):
        i, j = n // 8, lax.rem(n, 8)
        rows_s[count] = i
        cols_s[count] = j
        taken = (j <= first + i) & (mask[first + i, j] == 1)
        return count + taken.astype(jnp.int32)

    count = lax.fori_loop(0, 32, listed, 0)
    for extra in range(3):
        rows_s[count + extra] = 3
        cols_s[count + extra] = first + 3

    l_s[...] = jnp.zeros_like(l_s)
    acc_s[...] = jnp.zeros_like(acc_s)
    for copy in copies:
        copy.wait()

    @pl.when(c == 1)
    def _():
        for copy in others:
            copy.wait()

    scale = LOG2E / math.sqrt(HD)

    def scores(t, ref):
        ref[...] = lax.dot_general(
            k_s[cols_s[t]], q_s[rows_s[t]], (((1,), (1,)), ((), ())), preferred_element_type=jnp.float32
        )

    def step(t, now, later):
        i, j = rows_s[t], cols_s[t]
        fresh = (t == 0) | (rows_s[jnp.maximum(t - 1, 0)] != i)
        scores(t + 1, later)
        old = jnp.where(fresh, NEGATIVE_FILL, m_s[...])
        s = now[...]
        m = jnp.maximum(old, jnp.max(s, axis=0, keepdims=True) * scale)
        p = jnp.exp2(s * scale - m)
        fix = jnp.exp2(old - m)
        m_s[...] = m
        l = l_s[...] * fix + jnp.sum(p, axis=0, keepdims=True)
        l_s[...] = l
        acc = acc_s[...] * fix + jnp.dot(vt_s[j], p.astype(jnp.bfloat16), preferred_element_type=jnp.float32)
        acc_s[...] = acc

        @pl.when((j == first + i) & (t < count))
        def _():
            done = acc_s[...] / l_s[...]
            for n in range(BLOCK // HD):
                tile = slice(n * HD, (n + 1) * HD)
                out_t[i, tile] = done[:, tile].astype(jnp.bfloat16)
            out[lax.rem(i - z + 4, 4)] = done.T.astype(jnp.bfloat16)

    scores(0, sa_s)

    def two(u, _):
        step(2 * u, sa_s, sb_s)
        step(2 * u + 1, sb_s, sa_s)
        return 0

    lax.fori_loop(0, (count + 1) // 2, two, 0)


def attend(place, mask, own, other):
    vmem = pl.BlockSpec(memory_space=pltpu.VMEM)
    return pl.pallas_call(
        _attend_kernel,
        out_shape=(
            jax.ShapeDtypeStruct((4, BLOCK, HD), jnp.bfloat16),
            jax.ShapeDtypeStruct((4, BLOCK, HD), jnp.bfloat16),
        ),
        in_specs=[SMEM, SMEM, ANY, ANY],
        out_specs=(vmem, vmem),
        scratch_shapes=[
            pltpu.VMEM((4, BLOCK, HD), jnp.bfloat16),
            pltpu.VMEM((8, BLOCK, HD), jnp.bfloat16),
            pltpu.VMEM((8, HD, BLOCK), jnp.bfloat16),
            pltpu.VMEM((BLOCK, BLOCK), jnp.float32),
            pltpu.VMEM((BLOCK, BLOCK), jnp.float32),
            pltpu.VMEM((1, BLOCK), jnp.float32),
            pltpu.VMEM((1, BLOCK), jnp.float32),
            pltpu.VMEM((HD, BLOCK), jnp.float32),
            pltpu.SMEM((40,), jnp.int32),
            pltpu.SMEM((40,), jnp.int32),
            pltpu.SemaphoreType.DMA((24,)),
            pltpu.SemaphoreType.DMA((20,)),
        ],
        compiler_params=_params(VMEM_MIB),
        cost_estimate=pl.CostEstimate(
            flops=20 * 4 * BLOCK * BLOCK * HD,
            bytes_accessed=4 * MIB,
            transcendentals=20 * BLOCK * BLOCK,
        ),
        name="attend",
    )(place, mask, own, other)


def _mix_kernel(heads, added, place, *refs):
    count = 4 * len(heads)
    parts, (w_own, w_other) = refs[:count], refs[count : count + 2]
    sums = refs[count + 2] if added else None
    out = refs[count + 2 + added]
    a_s, w_s, sum_s, a_sem, w_sem = refs[count + 3 + added :]
    x, y, c, z = place[0], place[1], place[2], place[3]
    depth = len(heads) * HD

    def attended(n, side):
        return pltpu.make_async_copy(
            parts[4 * n + side], a_s.at[side, :, n], a_sem.at[4 * n + side]
        )

    def weight(side, block, ref):
        xx = lax.rem(x + side % 2, 2)
        from_z = lax.rem(z - block + 4, 4)
        at = pl.multiple_of((6 * from_z + 3 * xx + heads[0]) * HD, HD)
        return pltpu.make_async_copy(
            ref.at[pl.ds(at, depth)],
            w_s.at[pl.ds((4 * side + block) * depth, depth)],
            w_sem.at[4 * side + block],
        )

    def fetch(side):
        yy = lax.rem(y + side // 2, 2)
        for n in range(len(heads)):
            attended(n, side).start()
        for block in range(4):
            pl.when(yy == c)(weight(side, block, w_own).start)
            pl.when(yy != c)(weight(side, block, w_other).start)

    fetch(0)
    fetch(1)
    width = 512
    piece = 4 * depth
    for side in range(4):
        if 0 < side < 3:
            fetch(side + 1)
        for n in range(len(heads)):
            attended(n, side).wait()
        for block in range(4):
            weight(side, block, w_own).wait()

        def tile(t, _, side=side):
            cut = pl.ds(pl.multiple_of(t * width, width), width)
            rows = jnp.concatenate(
                [a_s[side, block, n] for block in range(4) for n in range(len(heads))], axis=1
            )
            term = jnp.dot(
                rows, w_s[side * piece : (side + 1) * piece, cut], preferred_element_type=jnp.float32
            )
            if side > 0:
                term += sum_s[:, cut]
            elif added:
                term += sums[:, cut]
            if side < 3:
                sum_s[:, cut] = term
            else:
                out[:, cut] = term.astype(out.dtype)
            return 0

        lax.fori_loop(0, out.shape[1] // width, tile, 0)


def mix(place, head, parts, w_own, w_other, sums, kind):
    heads = (head,)
    columns = w_own.shape[1]
    depth = 16 * len(heads) * HD
    vmem = pl.BlockSpec(memory_space=pltpu.VMEM)
    added = [] if sums is None else [sums]
    return pl.pallas_call(
        functools.partial(_mix_kernel, heads, len(added)),
        out_shape=jax.ShapeDtypeStruct((BLOCK, columns), kind),
        in_specs=[SMEM] + [ANY] * (len(parts) + 2) + [vmem] * len(added),
        out_specs=vmem,
        scratch_shapes=[
            pltpu.VMEM((4, 4, len(heads), BLOCK, HD), jnp.bfloat16),
            pltpu.VMEM((depth, columns), jnp.bfloat16),
            pltpu.VMEM((BLOCK, columns), jnp.float32),
            pltpu.SemaphoreType.DMA((4 * len(heads),)),
            pltpu.SemaphoreType.DMA((16,)),
        ],
        compiler_params=_params(VMEM_MIB),
        cost_estimate=pl.CostEstimate(
            flops=2 * BLOCK * depth * columns, bytes_accessed=9 * len(heads) * MIB, transcendentals=0
        ),
        name="mix",
    )(place, *parts, w_own, w_other, *added)


def _grad_kernel(count, place, *refs):
    parts, cot = refs[: 4 * count], refs[4 * count]
    sent, kept, left, right, l_sem, r_sem = refs[4 * count + 1 :]
    x, y, c = place[0], place[1], place[2]
    step = pl.program_id(0)

    @pl.when(step == 0)
    def _():
        rows = pltpu.make_async_copy(cot, right, r_sem)
        rows.start()
        for n, ref in enumerate(parts):
            head, dx, dy = n // 4, n % 2, n // 2 % 2
            mine = (lax.rem(y + dy, 2) == c).astype(jnp.int32)
            at = 2 * count * mine + count * lax.rem(x + dx, 2) + head
            pltpu.make_async_copy(ref, left.at[at], l_sem.at[at]).start()
        rows.wait()

    for n in range(count):
        at = count * step + n
        pltpu.make_async_copy(parts[n], left.at[at], l_sem.at[at]).wait()
    rows = jnp.concatenate(
        [
            jnp.concatenate(
                [
                    left[count * step + n, block, tile * HD : (tile + 1) * HD]
                    for block in range(4)
                    for tile in range(BLOCK // HD)
                ],
                axis=1,
            )
            for n in range(count)
        ]
    )
    total = jnp.dot(rows, right[...], preferred_element_type=jnp.float32)

    @pl.when(step < 2)
    def _():
        sent[...] = total.astype(jnp.bfloat16)

    @pl.when(step >= 2)
    def _():
        kept[...] = total


def grad(place, parts, cot):
    count = len(parts) // 4
    rows = count * HD
    tokens, width = cot.shape
    return pl.pallas_call(
        functools.partial(_grad_kernel, count),
        grid=(4,),
        out_shape=(
            jax.ShapeDtypeStruct((2 * rows, width), jnp.bfloat16),
            jax.ShapeDtypeStruct((2 * rows, width), jnp.float32),
        ),
        in_specs=[SMEM] + [ANY] * (len(parts) + 1),
        out_specs=(
            pl.BlockSpec((rows, width), lambda i: (jnp.minimum(i, 1), 0)),
            pl.BlockSpec((rows, width), lambda i: (jnp.maximum(i - 2, 0), 0)),
        ),
        scratch_shapes=[
            pltpu.VMEM((4 * count, 4, BLOCK, HD), jnp.bfloat16),
            pltpu.VMEM((tokens, width), jnp.bfloat16),
            pltpu.SemaphoreType.DMA((4 * count,)),
            pltpu.SemaphoreType.DMA,
        ],
        compiler_params=_params(VMEM_MIB),
        cost_estimate=pl.CostEstimate(
            flops=8 * rows * tokens * width, bytes_accessed=(4 * count + 3) * MIB, transcendentals=0
        ),
        name="grad",
    )(place, *parts, cot)


X_SWAP = [(0, 1), (1, 0), (2, 3), (3, 2)]
Y_SWAP = [(0, 2), (2, 0), (1, 3), (3, 1)]


OTHER_CORE = [(0, 1), (1, 0)]


def around(shift):
    return [(i, (i + shift) % 4) for i in range(4)]


def over_row(a, x_first):
    first, second = (X_SWAP, Y_SWAP) if x_first else (Y_SWAP, X_SWAP)
    near = lax.ppermute(a, "row", first)
    far = lax.ppermute(near, "row", second)
    next_to = lax.ppermute(a, "row", second)
    return [a, near, next_to, far] if x_first else [a, next_to, near, far]


def planes_body(queries, keys, values, out_weight, cotangent, block_mask):
    row, c, z = lax.axis_index("row"), lax.axis_index("col"), lax.axis_index("ctx")
    x, y = row % 2, row // 2
    place = jnp.stack([x, y, c, z]).astype(jnp.int32)
    columns = cotangent.shape[1]
    cut = columns // 2

    def exchanged(h, place):
        send, keep = pack(h, place, queries, keys, values)
        got = lax.ppermute(send, "row", X_SWAP)
        return keep, got

    def over_ctx(kept, got):
        pieces = [jnp.where(x == 0, kept, got), jnp.where(x == 0, got, kept)]
        return lax.all_to_all(jnp.concatenate(pieces), "ctx", 0, 0, tiled=True)

    def attended(h, own, before):
        other = lax.ppermute(own[:, 1:], "col", [(0, 1)])
        other, before = lax.optimization_barrier((other, before))
        out, out_t = attend(place, block_mask, own, other)
        home = [lax.ppermute(out[s], "ctx", around(s)) for s in range(1, 4)]
        return jnp.stack([out[0]] + home), over_row(out_t, True), before

    first_cot = lax.all_gather(cotangent[:, :cut], "ctx", axis=0, tiled=True)
    pair = exchanged(0, place)
    pair, later = lax.optimization_barrier((pair, place))
    own0 = over_ctx(*pair)
    pairs = [exchanged(h, later) for h in range(1, HALF)]
    w_other = lax.ppermute(out_weight, "col", OTHER_CORE)
    own0, pairs, w_other, first_cot = lax.optimization_barrier((own0, pairs, w_other, first_cot))
    own1 = over_ctx(*pairs[0])
    home0, grad0, _ = attended(0, own0, ())
    own1, pair, home0, grad0 = lax.optimization_barrier((own1, pairs[1], home0, grad0))
    own2 = over_ctx(*pair)
    home1, grad1, _ = attended(1, own1, ())
    mix0 = over_row(home0, False)
    own2, last_half, home1, mix0, grad1 = lax.optimization_barrier(
        (own2, cotangent[:, cut:], home1, mix0, grad1)
    )
    last_cot = lax.all_gather(last_half, "ctx", axis=0, tiled=True)
    mix1 = over_row(home1, False)
    home2, grad2, _ = attended(2, own2, ())
    sums = mix(place, 0, mix0, out_weight, w_other, None, jnp.float32)
    home2, mix1, sums = lax.optimization_barrier((home2, mix1, sums))
    mix2 = over_row(home2, False)

    def summed(parts, cot):
        sent, kept = grad(place, parts, cot)
        received = lax.ppermute(sent, "col", OTHER_CORE)
        done = (kept + received.astype(jnp.float32)).astype(jnp.bfloat16)
        return done.reshape(2, -1, cot.shape[1])

    early = summed(grad0 + grad1, first_cot)
    sums = mix(place, 1, mix1, out_weight, w_other, sums, jnp.float32)
    late = summed(grad2, first_cot)
    mixed_out = mix(place, 2, mix2, out_weight, w_other, sums, jnp.bfloat16)
    last = summed(grad0 + grad1 + grad2, last_cot)
    grad_weight = jnp.concatenate([jnp.concatenate([early, late], axis=1), last], axis=2)
    grad_weight = grad_weight.reshape(-1, columns)
    return (mixed_out, grad_weight)


def solution(mesh):
    in_specs = (
        P(("col", "ctx"), "row"),
        P(("col", "ctx"), "row"),
        P(("col", "ctx"), "row"),
        P("col", "row"),
        P(("col", "ctx"), "row"),
        P(),
    )
    out_specs = (P(("col", "ctx"), "row"), P(("col", "ctx"), "row"))
    four = dict(mesh.shape) == {"row": 4, "col": 2, "ctx": 4}

    def whole(queries, keys, values, out_weight, cotangent, block_mask):
        fits = queries.shape == (8 * BLOCK, 48 * HD)
        body = planes_body if four and fits else gathered_body
        mapped = jax.shard_map(
            body, mesh=mesh, in_specs=in_specs, out_specs=out_specs, check_vma=False
        )
        return mapped(queries, keys, values, out_weight, cotangent, block_mask)

    return whole
```

```python
import functools
import math

import jax
import jax.numpy as jnp
from jax import lax
from jax.experimental import pallas as pl
from jax.experimental.pallas import tpu as pltpu
from jax.sharding import PartitionSpec as P

HD = 128
BLOCK = 512
NEGATIVE_FILL = -1e30
HALF = 3
LOG2E = math.log2(math.e)
MIB = 1 << 20
VMEM_MIB = 56
ANY = pl.BlockSpec(memory_space=pl.ANY)
SMEM = pl.BlockSpec(memory_space=pltpu.SMEM)


def attend_block(carried, query_heads, key_block, value_block, allowed, score_scale):
    run_max, run_sum, weighted = carried
    tok_rows, head_count, head_size = query_heads.shape
    key_heads = key_block.reshape(key_block.shape[0], head_count, head_size)
    value_heads = value_block.reshape(value_block.shape[0], head_count, head_size)
    scores = (
        jnp.einsum("thd,uhd->thu", query_heads, key_heads, preferred_element_type=jnp.float32)
        * score_scale
    )
    scores = jnp.where(allowed[:, None, None], scores, NEGATIVE_FILL)
    new_max = jnp.maximum(run_max, jnp.max(scores, axis=2))
    correction = jnp.exp(run_max - new_max)
    weights = jnp.where(allowed[:, None, None], jnp.exp(scores - new_max[:, :, None]), 0.0)
    new_sum = run_sum * correction + jnp.sum(weights, axis=2)
    product = jnp.einsum(
        "thu,uhd->thd",
        weights.astype(jnp.bfloat16),
        value_heads,
        preferred_element_type=jnp.float32,
    )
    new_weighted = weighted * correction[:, :, None] + product
    return (new_max, new_sum, new_weighted)


def gathered_body(queries, keys, values, out_weight, cotangent, block_mask):
    tok_rows, feature_width = queries.shape
    head_count = feature_width // HD
    query_heads = queries.reshape(tok_rows, head_count, HD)
    score_scale = 1.0 / math.sqrt(HD)
    local_blocks = tok_rows // BLOCK
    first_block = lax.axis_index(("col", "ctx")) * local_blocks
    local_mask = lax.dynamic_slice_in_dim(block_mask, first_block, local_blocks, 0)
    start_state = (
        jnp.full((tok_rows, head_count), NEGATIVE_FILL, jnp.float32),
        jnp.zeros((tok_rows, head_count), jnp.float32),
        jnp.zeros((tok_rows, head_count, HD), jnp.float32),
    )
    key_piece = lax.all_gather(keys, ("col", "ctx"), axis=0, tiled=True)
    value_piece = lax.all_gather(values, ("col", "ctx"), axis=0, tiled=True)
    block_count = key_piece.shape[0] // BLOCK
    key_stack = key_piece.reshape(block_count, BLOCK, feature_width)
    value_stack = value_piece.reshape(block_count, BLOCK, feature_width)
    block_columns = jnp.arange(block_count, dtype=jnp.int32)

    def one_block(state_in, entries):
        key_block, value_block, block_column = entries
        mask_column = lax.dynamic_index_in_dim(local_mask, block_column, 1, keepdims=False)
        allowed = jnp.repeat(mask_column, BLOCK, total_repeat_length=tok_rows) == 1
        updated = attend_block(state_in, query_heads, key_block, value_block, allowed, score_scale)
        return (updated, None)

    state_out, _ = lax.scan(one_block, start_state, (key_stack, value_stack, block_columns))
    run_max, run_sum, weighted = state_out
    attended = (
        (weighted / run_sum[:, :, None]).reshape(tok_rows, feature_width).astype(jnp.bfloat16)
    )
    all_heads = lax.all_gather(attended, "row", axis=1, tiled=True)
    mixed_out = jnp.dot(
        all_heads,
        lax.all_gather(out_weight, "col", axis=0, tiled=True),
        preferred_element_type=jnp.float32,
    )
    grad_weight = lax.psum_scatter(
        lax.dot_general(
            all_heads, cotangent, (((0,), (0,)), ((), ())), preferred_element_type=jnp.float32
        ),
        ("col", "ctx"),
        scatter_dimension=0,
        tiled=True,
    )
    return (mixed_out.astype(jnp.bfloat16), grad_weight.astype(jnp.bfloat16))


def _params(mib):
    return pltpu.CompilerParams(vmem_limit_bytes=mib * MIB)


def _pack_kernel(place, *refs):
    columns, (send, keep) = refs[:6], refs[6:]
    for out, first in ((send, 0), (keep, 3)):
        out[0, 0] = columns[first][...]
        out[0, 1] = columns[first + 1][...]
        for n in range(BLOCK // HD):
            tile = slice(n * HD, (n + 1) * HD)
            out[0, 2, tile] = columns[first + 2][tile, :].T


def pack(head, place, q, k, v):
    shape = jax.ShapeDtypeStruct((2, 3, BLOCK, HD), jnp.bfloat16)

    def column(kept):
        def at(low, place_ref):
            side = place_ref[0] if kept else 1 - place_ref[0]
            return (0, 6 * low + 3 * side + head)

        return pl.BlockSpec((BLOCK, HD), at)

    out = pl.BlockSpec((1, 3, BLOCK, HD), lambda low, place_ref: (low, 0, 0, 0))
    return pl.pallas_call(
        _pack_kernel,
        grid_spec=pltpu.PrefetchScalarGridSpec(
            num_scalar_prefetch=1,
            grid=(2,),
            in_specs=[column(False)] * 3 + [column(True)] * 3,
            out_specs=(out, out),
        ),
        out_shape=(shape, shape),
        cost_estimate=pl.CostEstimate(flops=0, bytes_accessed=3 * MIB, transcendentals=0),
        name="pack",
    )(place, q, k, v, q, k, v)


def _attend_kernel(place, mask, *refs):
    own, other = refs[0], refs[1]
    out, out_t = refs[2:4]
    q_s, k_s, vt_s, sa_s, sb_s, m_s, l_s, acc_s, rows_s, cols_s, sems, other_sems = refs[4:]
    c, z = place[2], place[3]
    first = 4 * c
    copies = []
    others = []
    for s in range(4):
        b = s
        copies.append(pltpu.make_async_copy(own.at[s, 0], q_s.at[b], sems.at[2 * s]))
        copies.append(pltpu.make_async_copy(own.at[s, 1], k_s.at[first + b], sems.at[2 * s + 1]))
        for n in range(4):
            tile = pl.ds(n * HD, HD)
            copies.append(
                pltpu.make_async_copy(
                    own.at[s, 2, tile], vt_s.at[first + b, :, tile], sems.at[8 + 4 * s + n]
                )
            )
        others.append(pltpu.make_async_copy(other.at[s, 0], k_s.at[b], other_sems.at[s]))
        for n in range(4):
            tile = pl.ds(n * HD, HD)
            others.append(
                pltpu.make_async_copy(
                    other.at[s, 1, tile], vt_s.at[b, :, tile], other_sems.at[4 + 4 * s + n]
                )
            )
    for copy in copies:
        copy.start()

    @pl.when(c == 1)
    def _():
        for copy in others:
            copy.start()

    def listed(n, count):
        i, j = n // 8, lax.rem(n, 8)
        rows_s[count] = i
        cols_s[count] = j
        taken = (j <= first + i) & (mask[first + i, j] == 1)
        return count + taken.astype(jnp.int32)

    count = lax.fori_loop(0, 32, listed, 0)
    for extra in range(3):
        rows_s[count + extra] = 3
        cols_s[count + extra] = first + 3

    l_s[...] = jnp.zeros_like(l_s)
    acc_s[...] = jnp.zeros_like(acc_s)
    for copy in copies:
        copy.wait()

    @pl.when(c == 1)
    def _():
        for copy in others:
            copy.wait()

    scale = LOG2E / math.sqrt(HD)

    def scores(t, ref):
        ref[...] = lax.dot_general(
            k_s[cols_s[t]], q_s[rows_s[t]], (((1,), (1,)), ((), ())), preferred_element_type=jnp.float32
        )

    def step(t, now, later):
        i, j = rows_s[t], cols_s[t]
        fresh = (t == 0) | (rows_s[jnp.maximum(t - 1, 0)] != i)
        scores(t + 1, later)
        old = jnp.where(fresh, NEGATIVE_FILL, m_s[...])
        s = now[...]
        m = jnp.maximum(old, jnp.max(s, axis=0, keepdims=True) * scale)
        p = jnp.exp2(s * scale - m)
        fix = jnp.exp2(old - m)
        m_s[...] = m
        l = l_s[...] * fix + jnp.sum(p, axis=0, keepdims=True)
        l_s[...] = l
        acc = acc_s[...] * fix + jnp.dot(vt_s[j], p.astype(jnp.bfloat16), preferred_element_type=jnp.float32)
        acc_s[...] = acc

        @pl.when((j == first + i) & (t < count))
        def _():
            done = acc_s[...] / l_s[...]
            for n in range(BLOCK // HD):
                tile = slice(n * HD, (n + 1) * HD)
                out_t[i, tile] = done[:, tile].astype(jnp.bfloat16)
            out[lax.rem(i - z + 4, 4)] = done.T.astype(jnp.bfloat16)

    scores(0, sa_s)

    def two(u, _):
        step(2 * u, sa_s, sb_s)
        step(2 * u + 1, sb_s, sa_s)
        return 0

    lax.fori_loop(0, (count + 1) // 2, two, 0)


def attend(place, mask, own, other):
    vmem = pl.BlockSpec(memory_space=pltpu.VMEM)
    return pl.pallas_call(
        _attend_kernel,
        out_shape=(
            jax.ShapeDtypeStruct((4, BLOCK, HD), jnp.bfloat16),
            jax.ShapeDtypeStruct((4, BLOCK, HD), jnp.bfloat16),
        ),
        in_specs=[SMEM, SMEM, ANY, ANY],
        out_specs=(vmem, vmem),
        scratch_shapes=[
            pltpu.VMEM((4, BLOCK, HD), jnp.bfloat16),
            pltpu.VMEM((8, BLOCK, HD), jnp.bfloat16),
            pltpu.VMEM((8, HD, BLOCK), jnp.bfloat16),
            pltpu.VMEM((BLOCK, BLOCK), jnp.float32),
            pltpu.VMEM((BLOCK, BLOCK), jnp.float32),
            pltpu.VMEM((1, BLOCK), jnp.float32),
            pltpu.VMEM((1, BLOCK), jnp.float32),
            pltpu.VMEM((HD, BLOCK), jnp.float32),
            pltpu.SMEM((40,), jnp.int32),
            pltpu.SMEM((40,), jnp.int32),
            pltpu.SemaphoreType.DMA((24,)),
            pltpu.SemaphoreType.DMA((20,)),
        ],
        compiler_params=_params(VMEM_MIB),
        cost_estimate=pl.CostEstimate(
            flops=20 * 4 * BLOCK * BLOCK * HD,
            bytes_accessed=4 * MIB,
            transcendentals=20 * BLOCK * BLOCK,
        ),
        name="attend",
    )(place, mask, own, other)


def _mix_kernel(heads, added, place, *refs):
    count = 4 * len(heads)
    parts, (w_own, w_other) = refs[:count], refs[count : count + 2]
    sums = refs[count + 2] if added else None
    out = refs[count + 2 + added]
    a_s, w_s, sum_s, a_sem, w_sem, s_sem = refs[count + 3 + added :]
    x, y, c, z = place[0], place[1], place[2], place[3]
    depth = len(heads) * HD

    def attended(n, side):
        return pltpu.make_async_copy(
            parts[4 * n + side], a_s.at[side, :, n], a_sem.at[4 * n + side]
        )

    def weight(side, block, ref):
        xx = lax.rem(x + side % 2, 2)
        from_z = lax.rem(z - block + 4, 4)
        at = pl.multiple_of((6 * from_z + 3 * xx + heads[0]) * HD, HD)
        return pltpu.make_async_copy(
            ref.at[pl.ds(at, depth)],
            w_s.at[pl.ds((4 * side + block) * depth, depth)],
            w_sem.at[4 * side + block],
        )

    def fetch(side):
        yy = lax.rem(y + side // 2, 2)
        for n in range(len(heads)):
            attended(n, side).start()
        for block in range(4):
            pl.when(yy == c)(weight(side, block, w_own).start)
            pl.when(yy != c)(weight(side, block, w_other).start)

    if added:
        known = pltpu.make_async_copy(sums, sum_s, s_sem)
        known.start()
    fetch(0)
    fetch(1)
    width = 512
    piece = 8 * depth
    for half in range(2):
        for side in (2 * half, 2 * half + 1):
            if half == 0:
                fetch(side + 2)
            for n in range(len(heads)):
                attended(n, side).wait()
            for block in range(4):
                weight(side, block, w_own).wait()
        if half == 0 and added:
            known.wait()

        def tile(t, _, half=half):
            cut = pl.ds(pl.multiple_of(t * width, width), width)
            rows = jnp.concatenate(
                [
                    a_s[side, block, n]
                    for side in (2 * half, 2 * half + 1)
                    for block in range(4)
                    for n in range(len(heads))
                ],
                axis=1,
            )
            term = jnp.dot(
                rows, w_s[half * piece : (half + 1) * piece, cut], preferred_element_type=jnp.float32
            )
            if half > 0 or added:
                term += sum_s[:, cut]
            if half == 0:
                sum_s[:, cut] = term
            else:
                out[:, cut] = term.astype(out.dtype)
            return 0

        lax.fori_loop(0, out.shape[1] // width, tile, 0)


def mix(place, heads, parts, w_own, w_other, sums, kind):
    columns = w_own.shape[1]
    depth = 16 * len(heads) * HD
    vmem = pl.BlockSpec(memory_space=pltpu.VMEM)
    added = [] if sums is None else [sums]
    return pl.pallas_call(
        functools.partial(_mix_kernel, heads, len(added)),
        out_shape=jax.ShapeDtypeStruct((BLOCK, columns), kind),
        in_specs=[SMEM] + [ANY] * (len(parts) + 2) + [ANY] * len(added),
        out_specs=vmem,
        scratch_shapes=[
            pltpu.VMEM((4, 4, len(heads), BLOCK, HD), jnp.bfloat16),
            pltpu.VMEM((depth, columns), jnp.bfloat16),
            pltpu.VMEM((BLOCK, columns), jnp.float32),
            pltpu.SemaphoreType.DMA((4 * len(heads),)),
            pltpu.SemaphoreType.DMA((16,)),
            pltpu.SemaphoreType.DMA,
        ],
        compiler_params=_params(VMEM_MIB),
        cost_estimate=pl.CostEstimate(
            flops=2 * BLOCK * depth * columns, bytes_accessed=9 * len(heads) * MIB, transcendentals=0
        ),
        name="mix",
    )(place, *parts, w_own, w_other, *added)


def _grad_kernel(count, place, *refs):
    parts, cot = refs[: 4 * count], refs[4 * count]
    sent, kept, left, right, l_sem, r_sem = refs[4 * count + 1 :]
    x, y, c = place[0], place[1], place[2]
    step = pl.program_id(0)

    @pl.when(step == 0)
    def _():
        rows = pltpu.make_async_copy(cot, right, r_sem)
        rows.start()

        def start(turn):
            for n, ref in enumerate(parts):
                head, dx, dy = n // 4, n % 2, n // 2 % 2
                mine = (lax.rem(y + dy, 2) == c).astype(jnp.int32)
                at = 2 * count * mine + count * lax.rem(x + dx, 2) + head
                copy = pltpu.make_async_copy(ref, left.at[at], l_sem.at[at])
                pl.when(mine == turn)(copy.start)

        start(0)
        rows.wait()
        start(1)

    for n in range(count):
        at = count * step + n
        pltpu.make_async_copy(parts[n], left.at[at], l_sem.at[at]).wait()
    rows = jnp.concatenate(
        [
            jnp.concatenate(
                [
                    left[count * step + n, block, tile * HD : (tile + 1) * HD]
                    for block in range(4)
                    for tile in range(BLOCK // HD)
                ],
                axis=1,
            )
            for n in range(count)
        ]
    )
    total = jnp.dot(rows, right[...], preferred_element_type=jnp.float32)

    @pl.when(step < 2)
    def _():
        sent[...] = total.astype(jnp.bfloat16)

    @pl.when(step >= 2)
    def _():
        kept[...] = total


def grad(place, parts, cot):
    count = len(parts) // 4
    rows = count * HD
    tokens, width = cot.shape
    return pl.pallas_call(
        functools.partial(_grad_kernel, count),
        grid=(4,),
        out_shape=(
            jax.ShapeDtypeStruct((2 * rows, width), jnp.bfloat16),
            jax.ShapeDtypeStruct((2 * rows, width), jnp.float32),
        ),
        in_specs=[SMEM] + [ANY] * (len(parts) + 1),
        out_specs=(
            pl.BlockSpec((rows, width), lambda i: (jnp.minimum(i, 1), 0)),
            pl.BlockSpec((rows, width), lambda i: (jnp.maximum(i - 2, 0), 0)),
        ),
        scratch_shapes=[
            pltpu.VMEM((4 * count, 4, BLOCK, HD), jnp.bfloat16),
            pltpu.VMEM((tokens, width), jnp.bfloat16),
            pltpu.SemaphoreType.DMA((4 * count,)),
            pltpu.SemaphoreType.DMA,
        ],
        compiler_params=_params(VMEM_MIB),
        cost_estimate=pl.CostEstimate(
            flops=8 * rows * tokens * width, bytes_accessed=(4 * count + 3) * MIB, transcendentals=0
        ),
        name="grad",
    )(place, *parts, cot)


X_SWAP = [(0, 1), (1, 0), (2, 3), (3, 2)]
Y_SWAP = [(0, 2), (2, 0), (1, 3), (3, 1)]


XY_SWAP = [(0, 3), (3, 0), (1, 2), (2, 1)]
OTHER_CORE = [(0, 1), (1, 0)]


def around(shift):
    return [(i, (i + shift) % 4) for i in range(4)]


def over_row(a, x_first=None):
    if x_first is None:
        return [a] + [lax.ppermute(a, "row", pairs) for pairs in (X_SWAP, Y_SWAP, XY_SWAP)]
    first, second = (X_SWAP, Y_SWAP) if x_first else (Y_SWAP, X_SWAP)
    near = lax.ppermute(a, "row", first)
    far = lax.ppermute(near, "row", second)
    next_to = lax.ppermute(a, "row", second)
    return [a, near, next_to, far] if x_first else [a, next_to, near, far]


def planes_body(queries, keys, values, out_weight, cotangent, block_mask):
    row, c, z = lax.axis_index("row"), lax.axis_index("col"), lax.axis_index("ctx")
    x, y = row % 2, row // 2
    place = jnp.stack([x, y, c, z]).astype(jnp.int32)
    columns = cotangent.shape[1]
    cut = columns // 2

    def exchanged(h, place):
        send, keep = pack(h, place, queries, keys, values)
        got = lax.ppermute(send, "row", X_SWAP)
        return keep, got

    def over_ctx(kept, got):
        pieces = [jnp.where(x == 0, kept, got), jnp.where(x == 0, got, kept)]
        return lax.all_to_all(jnp.concatenate(pieces), "ctx", 0, 0, tiled=True)

    def attended(h, own, beside):
        other = lax.ppermute(own[:, 1:], "col", [(0, 1)])
        out, out_t = attend(place, block_mask, own, other)
        out, out_t, beside = lax.optimization_barrier((out, out_t, beside))
        home = [lax.ppermute(out[s], "ctx", around(s)) for s in range(1, 4)]
        return jnp.stack([out[0]] + home), over_row(out_t, True if h < 2 else None), beside

    first_cot = lax.all_gather(cotangent[:, :cut], "ctx", axis=0, tiled=True)
    pair = exchanged(0, place)
    pair, later = lax.optimization_barrier((pair, place))
    own0 = over_ctx(*pair)
    pairs = [exchanged(h, later) for h in range(1, HALF)]
    w_other = lax.ppermute(out_weight, "col", OTHER_CORE)
    own0, pairs, w_other, first_cot = lax.optimization_barrier((own0, pairs, w_other, first_cot))
    own1 = over_ctx(*pairs[0])
    home0, grad0, _ = attended(0, own0, ())
    own1, pair, home0, grad0 = lax.optimization_barrier((own1, pairs[1], home0, grad0))
    own2 = over_ctx(*pair)
    home1, grad1, _ = attended(1, own1, ())
    mix0 = over_row(home0, False)
    own2, last_half, home1, mix0, grad1 = lax.optimization_barrier(
        (own2, cotangent[:, cut:], home1, mix0, grad1)
    )
    last_cot = lax.all_gather(last_half, "ctx", axis=0, tiled=True)
    mix1 = [home1, lax.ppermute(home1, "row", X_SWAP), lax.ppermute(home1, "row", Y_SWAP)]
    home2, grad2, mix1 = attended(2, own2, mix1)
    mix1.append(lax.ppermute(mix1[2], "row", X_SWAP))
    home2, mix1, grad2[1:3] = lax.optimization_barrier((home2, mix1, grad2[1:3]))
    early = grad(place, grad0 + grad1, first_cot)
    mix2 = over_row(home2)

    def summed(pairs):
        sent = jnp.concatenate([p[0].reshape(2, -1, cut) for p in pairs], axis=1)
        kept = jnp.concatenate([p[1].reshape(2, -1, cut) for p in pairs], axis=1)
        received = lax.ppermute(sent, "col", OTHER_CORE)
        return (kept + received.astype(jnp.float32)).astype(jnp.bfloat16)

    sums = mix(place, (0, 1), mix0 + mix1, out_weight, w_other, None, jnp.float32)
    sums, grad2 = lax.optimization_barrier((sums, grad2))
    sums, early, grad2 = lax.optimization_barrier((sums, early, grad2))
    late = grad(place, grad2, first_cot)
    mix2, last_cot = lax.optimization_barrier((mix2, last_cot))
    last = grad(place, grad0 + grad1 + grad2, last_cot)
    mixed_out = mix(place, (2,), mix2, out_weight, w_other, sums, jnp.bfloat16)
    grad_weight = jnp.concatenate([summed([early, late]), summed([last])], axis=2)
    grad_weight = grad_weight.reshape(-1, columns)
    return (mixed_out, grad_weight)


def solution(mesh):
    in_specs = (
        P(("col", "ctx"), "row"),
        P(("col", "ctx"), "row"),
        P(("col", "ctx"), "row"),
        P("col", "row"),
        P(("col", "ctx"), "row"),
        P(),
    )
    out_specs = (P(("col", "ctx"), "row"), P(("col", "ctx"), "row"))
    four = dict(mesh.shape) == {"row": 4, "col": 2, "ctx": 4}

    def whole(queries, keys, values, out_weight, cotangent, block_mask):
        fits = queries.shape == (8 * BLOCK, 48 * HD)
        body = planes_body if four and fits else gathered_body
        mapped = jax.shard_map(
            body, mesh=mesh, in_specs=in_specs, out_specs=out_specs, check_vma=False
        )
        return mapped(queries, keys, values, out_weight, cotangent, block_mask)

    return whole
```

```python
import functools
import math

import jax
import jax.numpy as jnp
from jax import lax
from jax.experimental import pallas as pl
from jax.experimental.pallas import tpu as pltpu
from jax.sharding import PartitionSpec as P

HD = 128
BLOCK = 512
NEGATIVE_FILL = -1e30
HALF = 3
LOG2E = math.log2(math.e)
MIB = 1 << 20
VMEM_MIB = 56
ANY = pl.BlockSpec(memory_space=pl.ANY)
SMEM = pl.BlockSpec(memory_space=pltpu.SMEM)


def attend_block(carried, query_heads, key_block, value_block, allowed, score_scale):
    run_max, run_sum, weighted = carried
    tok_rows, head_count, head_size = query_heads.shape
    key_heads = key_block.reshape(key_block.shape[0], head_count, head_size)
    value_heads = value_block.reshape(value_block.shape[0], head_count, head_size)
    scores = (
        jnp.einsum("thd,uhd->thu", query_heads, key_heads, preferred_element_type=jnp.float32)
        * score_scale
    )
    scores = jnp.where(allowed[:, None, None], scores, NEGATIVE_FILL)
    new_max = jnp.maximum(run_max, jnp.max(scores, axis=2))
    correction = jnp.exp(run_max - new_max)
    weights = jnp.where(allowed[:, None, None], jnp.exp(scores - new_max[:, :, None]), 0.0)
    new_sum = run_sum * correction + jnp.sum(weights, axis=2)
    product = jnp.einsum(
        "thu,uhd->thd",
        weights.astype(jnp.bfloat16),
        value_heads,
        preferred_element_type=jnp.float32,
    )
    new_weighted = weighted * correction[:, :, None] + product
    return (new_max, new_sum, new_weighted)


def gathered_body(queries, keys, values, out_weight, cotangent, block_mask):
    tok_rows, feature_width = queries.shape
    head_count = feature_width // HD
    query_heads = queries.reshape(tok_rows, head_count, HD)
    score_scale = 1.0 / math.sqrt(HD)
    local_blocks = tok_rows // BLOCK
    first_block = lax.axis_index(("col", "ctx")) * local_blocks
    local_mask = lax.dynamic_slice_in_dim(block_mask, first_block, local_blocks, 0)
    start_state = (
        jnp.full((tok_rows, head_count), NEGATIVE_FILL, jnp.float32),
        jnp.zeros((tok_rows, head_count), jnp.float32),
        jnp.zeros((tok_rows, head_count, HD), jnp.float32),
    )
    key_piece = lax.all_gather(keys, ("col", "ctx"), axis=0, tiled=True)
    value_piece = lax.all_gather(values, ("col", "ctx"), axis=0, tiled=True)
    block_count = key_piece.shape[0] // BLOCK
    key_stack = key_piece.reshape(block_count, BLOCK, feature_width)
    value_stack = value_piece.reshape(block_count, BLOCK, feature_width)
    block_columns = jnp.arange(block_count, dtype=jnp.int32)

    def one_block(state_in, entries):
        key_block, value_block, block_column = entries
        mask_column = lax.dynamic_index_in_dim(local_mask, block_column, 1, keepdims=False)
        allowed = jnp.repeat(mask_column, BLOCK, total_repeat_length=tok_rows) == 1
        updated = attend_block(state_in, query_heads, key_block, value_block, allowed, score_scale)
        return (updated, None)

    state_out, _ = lax.scan(one_block, start_state, (key_stack, value_stack, block_columns))
    run_max, run_sum, weighted = state_out
    attended = (
        (weighted / run_sum[:, :, None]).reshape(tok_rows, feature_width).astype(jnp.bfloat16)
    )
    all_heads = lax.all_gather(attended, "row", axis=1, tiled=True)
    mixed_out = jnp.dot(
        all_heads,
        lax.all_gather(out_weight, "col", axis=0, tiled=True),
        preferred_element_type=jnp.float32,
    )
    grad_weight = lax.psum_scatter(
        lax.dot_general(
            all_heads, cotangent, (((0,), (0,)), ((), ())), preferred_element_type=jnp.float32
        ),
        ("col", "ctx"),
        scatter_dimension=0,
        tiled=True,
    )
    return (mixed_out.astype(jnp.bfloat16), grad_weight.astype(jnp.bfloat16))


def _params(mib):
    return pltpu.CompilerParams(vmem_limit_bytes=mib * MIB)


def _pack_kernel(place, *refs):
    columns, (send, keep) = refs[:6], refs[6:]
    for out, first in ((send, 0), (keep, 3)):
        out[0, 0] = columns[first][...]
        out[0, 1] = columns[first + 1][...]
        for n in range(BLOCK // HD):
            tile = slice(n * HD, (n + 1) * HD)
            out[0, 2, tile] = columns[first + 2][tile, :].T


def pack(head, place, q, k, v):
    shape = jax.ShapeDtypeStruct((2, 3, BLOCK, HD), jnp.bfloat16)

    def column(kept):
        def at(low, place_ref):
            side = place_ref[0] if kept else 1 - place_ref[0]
            return (0, 6 * low + 3 * side + head)

        return pl.BlockSpec((BLOCK, HD), at)

    out = pl.BlockSpec((1, 3, BLOCK, HD), lambda low, place_ref: (low, 0, 0, 0))
    return pl.pallas_call(
        _pack_kernel,
        grid_spec=pltpu.PrefetchScalarGridSpec(
            num_scalar_prefetch=1,
            grid=(2,),
            in_specs=[column(False)] * 3 + [column(True)] * 3,
            out_specs=(out, out),
        ),
        out_shape=(shape, shape),
        cost_estimate=pl.CostEstimate(flops=0, bytes_accessed=3 * MIB, transcendentals=0),
        name="pack",
    )(place, q, k, v, q, k, v)


def _attend_kernel(place, mask, *refs):
    own, other = refs[0], refs[1]
    out, out_t = refs[2:4]
    q_s, k_s, vt_s, sa_s, sb_s, m_s, l_s, acc_s, rows_s, cols_s, sems, other_sems = refs[4:]
    c, z = place[2], place[3]
    first = 4 * c
    copies = []
    others = []
    for s in range(4):
        b = s
        copies.append(pltpu.make_async_copy(own.at[s, 0], q_s.at[b], sems.at[2 * s]))
        copies.append(pltpu.make_async_copy(own.at[s, 1], k_s.at[first + b], sems.at[2 * s + 1]))
        for n in range(4):
            tile = pl.ds(n * HD, HD)
            copies.append(
                pltpu.make_async_copy(
                    own.at[s, 2, tile], vt_s.at[first + b, :, tile], sems.at[8 + 4 * s + n]
                )
            )
        others.append(pltpu.make_async_copy(other.at[s, 0], k_s.at[b], other_sems.at[s]))
        for n in range(4):
            tile = pl.ds(n * HD, HD)
            others.append(
                pltpu.make_async_copy(
                    other.at[s, 1, tile], vt_s.at[b, :, tile], other_sems.at[4 + 4 * s + n]
                )
            )
    for copy in copies:
        copy.start()

    @pl.when(c == 1)
    def _():
        for copy in others:
            copy.start()

    def listed(n, count):
        i, j = n // 8, lax.rem(n, 8)
        rows_s[count] = i
        cols_s[count] = j
        taken = (j <= first + i) & (mask[first + i, j] == 1)
        return count + taken.astype(jnp.int32)

    count = lax.fori_loop(0, 32, listed, 0)
    for extra in range(3):
        rows_s[count + extra] = 3
        cols_s[count + extra] = first + 3

    l_s[...] = jnp.zeros_like(l_s)
    acc_s[...] = jnp.zeros_like(acc_s)
    for copy in copies:
        copy.wait()

    @pl.when(c == 1)
    def _():
        for copy in others:
            copy.wait()

    scale = LOG2E / math.sqrt(HD)

    def scores(t, ref):
        ref[...] = lax.dot_general(
            k_s[cols_s[t]], q_s[rows_s[t]], (((1,), (1,)), ((), ())), preferred_element_type=jnp.float32
        )

    def step(t, now, later):
        i, j = rows_s[t], cols_s[t]
        fresh = (t == 0) | (rows_s[jnp.maximum(t - 1, 0)] != i)
        scores(t + 1, later)
        old = jnp.where(fresh, NEGATIVE_FILL, m_s[...])
        s = now[...]
        m = jnp.maximum(old, jnp.max(s, axis=0, keepdims=True) * scale)
        p = jnp.exp2(s * scale - m)
        fix = jnp.exp2(old - m)
        m_s[...] = m
        l = l_s[...] * fix + jnp.sum(p, axis=0, keepdims=True)
        l_s[...] = l
        acc = acc_s[...] * fix + jnp.dot(vt_s[j], p.astype(jnp.bfloat16), preferred_element_type=jnp.float32)
        acc_s[...] = acc

        @pl.when((j == first + i) & (t < count))
        def _():
            done = acc_s[...] / l_s[...]
            for n in range(BLOCK // HD):
                tile = slice(n * HD, (n + 1) * HD)
                out_t[i, tile] = done[:, tile].astype(jnp.bfloat16)
            out[lax.rem(i - z + 4, 4)] = done.T.astype(jnp.bfloat16)

    scores(0, sa_s)

    def two(u, _):
        step(2 * u, sa_s, sb_s)
        step(2 * u + 1, sb_s, sa_s)
        return 0

    lax.fori_loop(0, (count + 1) // 2, two, 0)


def attend(place, mask, own, other):
    vmem = pl.BlockSpec(memory_space=pltpu.VMEM)
    return pl.pallas_call(
        _attend_kernel,
        out_shape=(
            jax.ShapeDtypeStruct((4, BLOCK, HD), jnp.bfloat16),
            jax.ShapeDtypeStruct((4, BLOCK, HD), jnp.bfloat16),
        ),
        in_specs=[SMEM, SMEM, ANY, ANY],
        out_specs=(vmem, vmem),
        scratch_shapes=[
            pltpu.VMEM((4, BLOCK, HD), jnp.bfloat16),
            pltpu.VMEM((8, BLOCK, HD), jnp.bfloat16),
            pltpu.VMEM((8, HD, BLOCK), jnp.bfloat16),
            pltpu.VMEM((BLOCK, BLOCK), jnp.float32),
            pltpu.VMEM((BLOCK, BLOCK), jnp.float32),
            pltpu.VMEM((1, BLOCK), jnp.float32),
            pltpu.VMEM((1, BLOCK), jnp.float32),
            pltpu.VMEM((HD, BLOCK), jnp.float32),
            pltpu.SMEM((40,), jnp.int32),
            pltpu.SMEM((40,), jnp.int32),
            pltpu.SemaphoreType.DMA((24,)),
            pltpu.SemaphoreType.DMA((20,)),
        ],
        compiler_params=_params(VMEM_MIB),
        cost_estimate=pl.CostEstimate(
            flops=20 * 4 * BLOCK * BLOCK * HD,
            bytes_accessed=4 * MIB,
            transcendentals=20 * BLOCK * BLOCK,
        ),
        name="attend",
    )(place, mask, own, other)


def _mix_kernel(heads, added, place, *refs):
    count = 4 * len(heads)
    parts, (w_own, w_other) = refs[:count], refs[count : count + 2]
    sums = refs[count + 2] if added else None
    out = refs[count + 2 + added]
    a_s, w_s, sum_s, a_sem, w_sem, s_sem = refs[count + 3 + added :]
    x, y, c, z = place[0], place[1], place[2], place[3]
    depth = len(heads) * HD

    def attended(n, side):
        return pltpu.make_async_copy(
            parts[4 * n + side], a_s.at[side, :, n], a_sem.at[4 * n + side]
        )

    def weight(side, block, ref):
        xx = lax.rem(x + side % 2, 2)
        from_z = lax.rem(z - block + 4, 4)
        at = pl.multiple_of((6 * from_z + 3 * xx + heads[0]) * HD, HD)
        return pltpu.make_async_copy(
            ref.at[pl.ds(at, depth)],
            w_s.at[pl.ds((4 * side + block) * depth, depth)],
            w_sem.at[4 * side + block],
        )

    def fetch(side):
        yy = lax.rem(y + side // 2, 2)
        for n in range(len(heads)):
            attended(n, side).start()
        for block in range(4):
            pl.when(yy == c)(weight(side, block, w_own).start)
            pl.when(yy != c)(weight(side, block, w_other).start)

    if added:
        known = pltpu.make_async_copy(sums, sum_s, s_sem)
        known.start()
    fetch(0)
    fetch(1)
    width = 512
    piece = 8 * depth
    for half in range(2):
        for side in (2 * half, 2 * half + 1):
            if half == 0:
                fetch(side + 2)
            for n in range(len(heads)):
                attended(n, side).wait()
            for block in range(4):
                weight(side, block, w_own).wait()
        if half == 0 and added:
            known.wait()

        def tile(t, _, half=half):
            cut = pl.ds(pl.multiple_of(t * width, width), width)
            rows = jnp.concatenate(
                [
                    a_s[side, block, n]
                    for side in (2 * half, 2 * half + 1)
                    for block in range(4)
                    for n in range(len(heads))
                ],
                axis=1,
            )
            term = jnp.dot(
                rows, w_s[half * piece : (half + 1) * piece, cut], preferred_element_type=jnp.float32
            )
            if half > 0 or added:
                term += sum_s[:, cut]
            if half == 0:
                sum_s[:, cut] = term
            else:
                out[:, cut] = term.astype(out.dtype)
            return 0

        lax.fori_loop(0, out.shape[1] // width, tile, 0)


def mix(place, heads, parts, w_own, w_other, sums, kind):
    columns = w_own.shape[1]
    depth = 16 * len(heads) * HD
    vmem = pl.BlockSpec(memory_space=pltpu.VMEM)
    added = [] if sums is None else [sums]
    return pl.pallas_call(
        functools.partial(_mix_kernel, heads, len(added)),
        out_shape=jax.ShapeDtypeStruct((BLOCK, columns), kind),
        in_specs=[SMEM] + [ANY] * (len(parts) + 2) + [ANY] * len(added),
        out_specs=vmem,
        scratch_shapes=[
            pltpu.VMEM((4, 4, len(heads), BLOCK, HD), jnp.bfloat16),
            pltpu.VMEM((depth, columns), jnp.bfloat16),
            pltpu.VMEM((BLOCK, columns), jnp.float32),
            pltpu.SemaphoreType.DMA((4 * len(heads),)),
            pltpu.SemaphoreType.DMA((16,)),
            pltpu.SemaphoreType.DMA,
        ],
        compiler_params=_params(VMEM_MIB),
        cost_estimate=pl.CostEstimate(
            flops=2 * BLOCK * depth * columns, bytes_accessed=9 * len(heads) * MIB, transcendentals=0
        ),
        name="mix",
    )(place, *parts, w_own, w_other, *added)


def _grad_kernel(count, place, *refs):
    parts, cot = refs[: 4 * count], refs[4 * count]
    sent, kept, left, right, l_sem, r_sem = refs[4 * count + 1 :]
    x, y, c = place[0], place[1], place[2]
    step = pl.program_id(0)

    @pl.when(step == 0)
    def _():
        rows = pltpu.make_async_copy(cot, right, r_sem)
        rows.start()

        def start(turn):
            for n, ref in enumerate(parts):
                head, dx, dy = n // 4, n % 2, n // 2 % 2
                mine = (lax.rem(y + dy, 2) == c).astype(jnp.int32)
                at = 2 * count * mine + count * lax.rem(x + dx, 2) + head
                copy = pltpu.make_async_copy(ref, left.at[at], l_sem.at[at])
                pl.when(mine == turn)(copy.start)

        start(0)
        rows.wait()
        start(1)

    for n in range(count):
        at = count * step + n
        pltpu.make_async_copy(parts[n], left.at[at], l_sem.at[at]).wait()
    rows = jnp.concatenate(
        [
            jnp.concatenate(
                [
                    left[count * step + n, block, tile * HD : (tile + 1) * HD]
                    for block in range(4)
                    for tile in range(BLOCK // HD)
                ],
                axis=1,
            )
            for n in range(count)
        ]
    )
    total = jnp.dot(rows, right[...], preferred_element_type=jnp.float32)

    @pl.when(step < 2)
    def _():
        sent[...] = total.astype(jnp.bfloat16)

    @pl.when(step >= 2)
    def _():
        kept[...] = total


def grad(place, parts, cot):
    count = len(parts) // 4
    rows = count * HD
    tokens, width = cot.shape
    return pl.pallas_call(
        functools.partial(_grad_kernel, count),
        grid=(4,),
        out_shape=(
            jax.ShapeDtypeStruct((2 * rows, width), jnp.bfloat16),
            jax.ShapeDtypeStruct((2 * rows, width), jnp.float32),
        ),
        in_specs=[SMEM] + [ANY] * (len(parts) + 1),
        out_specs=(
            pl.BlockSpec((rows, width), lambda i: (jnp.minimum(i, 1), 0)),
            pl.BlockSpec((rows, width), lambda i: (jnp.maximum(i - 2, 0), 0)),
        ),
        scratch_shapes=[
            pltpu.VMEM((4 * count, 4, BLOCK, HD), jnp.bfloat16),
            pltpu.VMEM((tokens, width), jnp.bfloat16),
            pltpu.SemaphoreType.DMA((4 * count,)),
            pltpu.SemaphoreType.DMA,
        ],
        compiler_params=_params(VMEM_MIB),
        cost_estimate=pl.CostEstimate(
            flops=8 * rows * tokens * width, bytes_accessed=(4 * count + 3) * MIB, transcendentals=0
        ),
        name="grad",
    )(place, *parts, cot)


X_SWAP = [(0, 1), (1, 0), (2, 3), (3, 2)]
Y_SWAP = [(0, 2), (2, 0), (1, 3), (3, 1)]


XY_SWAP = [(0, 3), (3, 0), (1, 2), (2, 1)]
OTHER_CORE = [(0, 1), (1, 0)]


def around(shift):
    return [(i, (i + shift) % 4) for i in range(4)]


def over_row(a, x_first=None):
    if x_first is None:
        return [a] + [lax.ppermute(a, "row", pairs) for pairs in (X_SWAP, Y_SWAP, XY_SWAP)]
    first, second = (X_SWAP, Y_SWAP) if x_first else (Y_SWAP, X_SWAP)
    near = lax.ppermute(a, "row", first)
    far = lax.ppermute(near, "row", second)
    next_to = lax.ppermute(a, "row", second)
    return [a, near, next_to, far] if x_first else [a, next_to, near, far]


def planes_body(queries, keys, values, out_weight, cotangent, block_mask):
    row, c, z = lax.axis_index("row"), lax.axis_index("col"), lax.axis_index("ctx")
    x, y = row % 2, row // 2
    place = jnp.stack([x, y, c, z]).astype(jnp.int32)
    columns = cotangent.shape[1]
    cut = columns // 2

    def exchanged(h, place):
        send, keep = pack(h, place, queries, keys, values)
        got = lax.ppermute(send, "row", X_SWAP)
        return keep, got

    def merged(kept, got):
        return jnp.concatenate([jnp.where(x == 0, kept, got), jnp.where(x == 0, got, kept)])

    def over_ctx(pieces):
        return lax.all_to_all(pieces, "ctx", 0, 0, tiled=True)

    def attended(h, own, beside):
        other = lax.ppermute(own[:, 1:], "col", [(0, 1)])
        out, out_t = attend(place, block_mask, own, other)
        out, out_t, beside = lax.optimization_barrier((out, out_t, beside))
        home = [lax.ppermute(out[s], "ctx", around(s)) for s in range(1, 4)]
        return jnp.stack([out[0]] + home), over_row(out_t, True if h < 2 else None), beside

    first_cot = lax.all_gather(cotangent[:, :cut], "ctx", axis=0, tiled=True)
    pair = exchanged(0, place)
    pair, later = lax.optimization_barrier((pair, place))
    own0 = over_ctx(merged(*pair))
    pairs = [exchanged(h, later) for h in range(1, HALF)]
    w_other = lax.ppermute(out_weight, "col", OTHER_CORE)
    one, two = [merged(*pair) for pair in pairs]
    own0, one, w_other, first_cot = lax.optimization_barrier((own0, one, w_other, first_cot))
    own1 = over_ctx(one)
    home0, grad0, _ = attended(0, own0, ())
    own1, two, home0, grad0 = lax.optimization_barrier((own1, two, home0, grad0))
    own2 = over_ctx(two)
    home1, grad1, _ = attended(1, own1, ())
    mix0 = over_row(home0, False)
    own2, last_half, home1, mix0, grad1 = lax.optimization_barrier(
        (own2, cotangent[:, cut:], home1, mix0, grad1)
    )
    last_cot = lax.all_gather(last_half, "ctx", axis=0, tiled=True)
    mix1 = [home1, lax.ppermute(home1, "row", X_SWAP), lax.ppermute(home1, "row", Y_SWAP)]
    home2, grad2, mix1 = attended(2, own2, mix1)
    mix1.append(lax.ppermute(mix1[2], "row", X_SWAP))
    home2, mix1, grad2[1:3] = lax.optimization_barrier((home2, mix1, grad2[1:3]))
    early = grad(place, grad0 + grad1, first_cot)

    def summed(pairs):
        sent = jnp.concatenate([p[0].reshape(2, -1, p[0].shape[1]) for p in pairs], axis=1)
        kept = jnp.concatenate([p[1].reshape(2, -1, p[1].shape[1]) for p in pairs], axis=1)
        received = lax.ppermute(sent, "col", OTHER_CORE)
        return (kept + received.astype(jnp.float32)).astype(jnp.bfloat16)

    sums = mix(place, (0, 1), mix0 + mix1, out_weight, w_other, None, jnp.float32)
    mix2 = over_row(home2)
    sums, grad2 = lax.optimization_barrier((sums, grad2))
    sums, early, grad2 = lax.optimization_barrier((sums, early, grad2))
    late = grad(place, grad2, first_cot)
    mix2, last_cot = lax.optimization_barrier((mix2, last_cot))
    last = grad(place, grad0 + grad1 + grad2, last_cot)
    mixed_out = mix(place, (2,), mix2, out_weight, w_other, sums, jnp.bfloat16)
    grad_weight = jnp.concatenate([summed([early, late]), summed([last])], axis=2)
    grad_weight = grad_weight.reshape(-1, columns)
    return (mixed_out, grad_weight)


def solution(mesh):
    in_specs = (
        P(("col", "ctx"), "row"),
        P(("col", "ctx"), "row"),
        P(("col", "ctx"), "row"),
        P("col", "row"),
        P(("col", "ctx"), "row"),
        P(),
    )
    out_specs = (P(("col", "ctx"), "row"), P(("col", "ctx"), "row"))
    four = dict(mesh.shape) == {"row": 4, "col": 2, "ctx": 4}

    def whole(queries, keys, values, out_weight, cotangent, block_mask):
        fits = queries.shape == (8 * BLOCK, 48 * HD)
        body = planes_body if four and fits else gathered_body
        mapped = jax.shard_map(
            body, mesh=mesh, in_specs=in_specs, out_specs=out_specs, check_vma=False
        )
        return mapped(queries, keys, values, out_weight, cotangent, block_mask)

    return whole
```

```python
import functools
import math

import jax
import jax.numpy as jnp
from jax import lax
from jax.experimental import pallas as pl
from jax.experimental.pallas import tpu as pltpu
from jax.sharding import PartitionSpec as P

HD = 128
BLOCK = 512
NEGATIVE_FILL = -1e30
HALF = 3
LOG2E = math.log2(math.e)
MIB = 1 << 20
VMEM_MIB = 56
ANY = pl.BlockSpec(memory_space=pl.ANY)
SMEM = pl.BlockSpec(memory_space=pltpu.SMEM)


def attend_block(carried, query_heads, key_block, value_block, allowed, score_scale):
    run_max, run_sum, weighted = carried
    tok_rows, head_count, head_size = query_heads.shape
    key_heads = key_block.reshape(key_block.shape[0], head_count, head_size)
    value_heads = value_block.reshape(value_block.shape[0], head_count, head_size)
    scores = (
        jnp.einsum("thd,uhd->thu", query_heads, key_heads, preferred_element_type=jnp.float32)
        * score_scale
    )
    scores = jnp.where(allowed[:, None, None], scores, NEGATIVE_FILL)
    new_max = jnp.maximum(run_max, jnp.max(scores, axis=2))
    correction = jnp.exp(run_max - new_max)
    weights = jnp.where(allowed[:, None, None], jnp.exp(scores - new_max[:, :, None]), 0.0)
    new_sum = run_sum * correction + jnp.sum(weights, axis=2)
    product = jnp.einsum(
        "thu,uhd->thd",
        weights.astype(jnp.bfloat16),
        value_heads,
        preferred_element_type=jnp.float32,
    )
    new_weighted = weighted * correction[:, :, None] + product
    return (new_max, new_sum, new_weighted)


def gathered_body(queries, keys, values, out_weight, cotangent, block_mask):
    tok_rows, feature_width = queries.shape
    head_count = feature_width // HD
    query_heads = queries.reshape(tok_rows, head_count, HD)
    score_scale = 1.0 / math.sqrt(HD)
    local_blocks = tok_rows // BLOCK
    first_block = lax.axis_index(("col", "ctx")) * local_blocks
    local_mask = lax.dynamic_slice_in_dim(block_mask, first_block, local_blocks, 0)
    start_state = (
        jnp.full((tok_rows, head_count), NEGATIVE_FILL, jnp.float32),
        jnp.zeros((tok_rows, head_count), jnp.float32),
        jnp.zeros((tok_rows, head_count, HD), jnp.float32),
    )
    key_piece = lax.all_gather(keys, ("col", "ctx"), axis=0, tiled=True)
    value_piece = lax.all_gather(values, ("col", "ctx"), axis=0, tiled=True)
    block_count = key_piece.shape[0] // BLOCK
    key_stack = key_piece.reshape(block_count, BLOCK, feature_width)
    value_stack = value_piece.reshape(block_count, BLOCK, feature_width)
    block_columns = jnp.arange(block_count, dtype=jnp.int32)

    def one_block(state_in, entries):
        key_block, value_block, block_column = entries
        mask_column = lax.dynamic_index_in_dim(local_mask, block_column, 1, keepdims=False)
        allowed = jnp.repeat(mask_column, BLOCK, total_repeat_length=tok_rows) == 1
        updated = attend_block(state_in, query_heads, key_block, value_block, allowed, score_scale)
        return (updated, None)

    state_out, _ = lax.scan(one_block, start_state, (key_stack, value_stack, block_columns))
    run_max, run_sum, weighted = state_out
    attended = (
        (weighted / run_sum[:, :, None]).reshape(tok_rows, feature_width).astype(jnp.bfloat16)
    )
    all_heads = lax.all_gather(attended, "row", axis=1, tiled=True)
    mixed_out = jnp.dot(
        all_heads,
        lax.all_gather(out_weight, "col", axis=0, tiled=True),
        preferred_element_type=jnp.float32,
    )
    grad_weight = lax.psum_scatter(
        lax.dot_general(
            all_heads, cotangent, (((0,), (0,)), ((), ())), preferred_element_type=jnp.float32
        ),
        ("col", "ctx"),
        scatter_dimension=0,
        tiled=True,
    )
    return (mixed_out.astype(jnp.bfloat16), grad_weight.astype(jnp.bfloat16))


def _params(mib):
    return pltpu.CompilerParams(vmem_limit_bytes=mib * MIB)


def _pack_kernel(place, *refs):
    columns, (send, keep) = refs[:6], refs[6:]
    for out, first in ((send, 0), (keep, 3)):
        out[0, 0] = columns[first][...]
        out[0, 1] = columns[first + 1][...]
        for n in range(BLOCK // HD):
            tile = slice(n * HD, (n + 1) * HD)
            out[0, 2, tile] = columns[first + 2][tile, :].T


def pack(head, place, q, k, v):
    shape = jax.ShapeDtypeStruct((2, 3, BLOCK, HD), jnp.bfloat16)

    def column(kept):
        def at(low, place_ref):
            side = place_ref[0] if kept else 1 - place_ref[0]
            return (0, 6 * low + 3 * side + head)

        return pl.BlockSpec((BLOCK, HD), at)

    out = pl.BlockSpec((1, 3, BLOCK, HD), lambda low, place_ref: (low, 0, 0, 0))
    return pl.pallas_call(
        _pack_kernel,
        grid_spec=pltpu.PrefetchScalarGridSpec(
            num_scalar_prefetch=1,
            grid=(2,),
            in_specs=[column(False)] * 3 + [column(True)] * 3,
            out_specs=(out, out),
        ),
        out_shape=(shape, shape),
        cost_estimate=pl.CostEstimate(flops=0, bytes_accessed=3 * MIB, transcendentals=0),
        name="pack",
    )(place, q, k, v, q, k, v)


def _attend_kernel(place, mask, *refs):
    own, other = refs[0], refs[1]
    out, out_t = refs[2:4]
    q_s, k_s, vt_s, sa_s, sb_s, m_s, l_s, acc_s, rows_s, cols_s, sems, other_sems = refs[4:]
    c, z = place[2], place[3]
    first = 4 * c
    copies = []
    others = []
    for s in range(4):
        b = s
        copies.append(pltpu.make_async_copy(own.at[s, 0], q_s.at[b], sems.at[2 * s]))
        copies.append(pltpu.make_async_copy(own.at[s, 1], k_s.at[first + b], sems.at[2 * s + 1]))
        for n in range(4):
            tile = pl.ds(n * HD, HD)
            copies.append(
                pltpu.make_async_copy(
                    own.at[s, 2, tile], vt_s.at[first + b, :, tile], sems.at[8 + 4 * s + n]
                )
            )
        others.append(pltpu.make_async_copy(other.at[s, 0], k_s.at[b], other_sems.at[s]))
        for n in range(4):
            tile = pl.ds(n * HD, HD)
            others.append(
                pltpu.make_async_copy(
                    other.at[s, 1, tile], vt_s.at[b, :, tile], other_sems.at[4 + 4 * s + n]
                )
            )
    for copy in copies:
        copy.start()

    @pl.when(c == 1)
    def _():
        for copy in others:
            copy.start()

    def listed(n, count):
        i, j = n // 8, lax.rem(n, 8)
        rows_s[count] = i
        cols_s[count] = j
        taken = (j <= first + i) & (mask[first + i, j] == 1)
        return count + taken.astype(jnp.int32)

    count = lax.fori_loop(0, 32, listed, 0)
    for extra in range(3):
        rows_s[count + extra] = 3
        cols_s[count + extra] = first + 3

    l_s[...] = jnp.zeros_like(l_s)
    acc_s[...] = jnp.zeros_like(acc_s)
    for copy in copies:
        copy.wait()

    @pl.when(c == 1)
    def _():
        for copy in others:
            copy.wait()

    scale = LOG2E / math.sqrt(HD)

    def scores(t, ref):
        ref[...] = lax.dot_general(
            k_s[cols_s[t]], q_s[rows_s[t]], (((1,), (1,)), ((), ())), preferred_element_type=jnp.float32
        )

    def step(t, now, later):
        i, j = rows_s[t], cols_s[t]
        fresh = (t == 0) | (rows_s[jnp.maximum(t - 1, 0)] != i)
        scores(t + 1, later)
        old = jnp.where(fresh, NEGATIVE_FILL, m_s[...])
        s = now[...]
        m = jnp.maximum(old, jnp.max(s, axis=0, keepdims=True) * scale)
        p = jnp.exp2(s * scale - m)
        fix = jnp.exp2(old - m)
        m_s[...] = m
        l = l_s[...] * fix + jnp.sum(p, axis=0, keepdims=True)
        l_s[...] = l
        acc = acc_s[...] * fix + jnp.dot(vt_s[j], p.astype(jnp.bfloat16), preferred_element_type=jnp.float32)
        acc_s[...] = acc

        @pl.when((j == first + i) & (t < count))
        def _():
            done = acc_s[...] / l_s[...]
            for n in range(BLOCK // HD):
                tile = slice(n * HD, (n + 1) * HD)
                out_t[i, tile] = done[:, tile].astype(jnp.bfloat16)
            out[lax.rem(i - z + 4, 4)] = done.T.astype(jnp.bfloat16)

    scores(0, sa_s)

    def two(u, _):
        step(2 * u, sa_s, sb_s)
        step(2 * u + 1, sb_s, sa_s)
        return 0

    lax.fori_loop(0, (count + 1) // 2, two, 0)


def attend(place, mask, own, other):
    vmem = pl.BlockSpec(memory_space=pltpu.VMEM)
    return pl.pallas_call(
        _attend_kernel,
        out_shape=(
            jax.ShapeDtypeStruct((4, BLOCK, HD), jnp.bfloat16),
            jax.ShapeDtypeStruct((4, BLOCK, HD), jnp.bfloat16),
        ),
        in_specs=[SMEM, SMEM, ANY, ANY],
        out_specs=(vmem, vmem),
        scratch_shapes=[
            pltpu.VMEM((4, BLOCK, HD), jnp.bfloat16),
            pltpu.VMEM((8, BLOCK, HD), jnp.bfloat16),
            pltpu.VMEM((8, HD, BLOCK), jnp.bfloat16),
            pltpu.VMEM((BLOCK, BLOCK), jnp.float32),
            pltpu.VMEM((BLOCK, BLOCK), jnp.float32),
            pltpu.VMEM((1, BLOCK), jnp.float32),
            pltpu.VMEM((1, BLOCK), jnp.float32),
            pltpu.VMEM((HD, BLOCK), jnp.float32),
            pltpu.SMEM((40,), jnp.int32),
            pltpu.SMEM((40,), jnp.int32),
            pltpu.SemaphoreType.DMA((24,)),
            pltpu.SemaphoreType.DMA((20,)),
        ],
        compiler_params=_params(VMEM_MIB),
        cost_estimate=pl.CostEstimate(
            flops=20 * 4 * BLOCK * BLOCK * HD,
            bytes_accessed=4 * MIB,
            transcendentals=20 * BLOCK * BLOCK,
        ),
        name="attend",
    )(place, mask, own, other)


def _mix_kernel(heads, sides, added, place, *refs):
    count = len(sides) * len(heads)
    parts, (w_own, w_other) = refs[:count], refs[count : count + 2]
    sums = refs[count + 2] if added else None
    out = refs[count + 2 + added]
    a_s, w_s, sum_s, a_sem, w_sem, s_sem = refs[count + 3 + added :]
    x, y, c, z = place[0], place[1], place[2], place[3]
    depth = len(heads) * HD

    def attended(n, side):
        return pltpu.make_async_copy(
            parts[len(sides) * n + side], a_s.at[side, :, n], a_sem.at[len(sides) * n + side]
        )

    def weight(side, block, ref):
        xx = lax.rem(x + sides[side] % 2, 2)
        from_z = lax.rem(z - block + 4, 4)
        at = pl.multiple_of((6 * from_z + 3 * xx + heads[0]) * HD, HD)
        return pltpu.make_async_copy(
            ref.at[pl.ds(at, depth)],
            w_s.at[pl.ds((4 * side + block) * depth, depth)],
            w_sem.at[4 * side + block],
        )

    def fetch(side):
        yy = lax.rem(y + sides[side] // 2, 2)
        for n in range(len(heads)):
            attended(n, side).start()
        for block in range(4):
            pl.when(yy == c)(weight(side, block, w_own).start)
            pl.when(yy != c)(weight(side, block, w_other).start)

    if added:
        known = pltpu.make_async_copy(sums, sum_s, s_sem)
        known.start()
    fetch(0)
    fetch(1)
    width = 512
    piece = 8 * depth
    halves = len(sides) // 2
    for half in range(halves):
        for side in (2 * half, 2 * half + 1):
            if half < halves - 1:
                fetch(side + 2)
            for n in range(len(heads)):
                attended(n, side).wait()
            for block in range(4):
                weight(side, block, w_own).wait()
        if half == 0 and added:
            known.wait()

        def tile(t, _, half=half):
            cut = pl.ds(pl.multiple_of(t * width, width), width)
            rows = jnp.concatenate(
                [
                    a_s[side, block, n]
                    for side in (2 * half, 2 * half + 1)
                    for block in range(4)
                    for n in range(len(heads))
                ],
                axis=1,
            )
            term = jnp.dot(
                rows, w_s[half * piece : (half + 1) * piece, cut], preferred_element_type=jnp.float32
            )
            if half > 0 or added:
                term += sum_s[:, cut]
            if half < halves - 1:
                sum_s[:, cut] = term
            else:
                out[:, cut] = term.astype(out.dtype)
            return 0

        lax.fori_loop(0, out.shape[1] // width, tile, 0)


def mix(place, heads, parts, w_own, w_other, sums, kind, sides=(0, 1, 2, 3)):
    columns = w_own.shape[1]
    depth = 4 * len(sides) * len(heads) * HD
    vmem = pl.BlockSpec(memory_space=pltpu.VMEM)
    added = [] if sums is None else [sums]
    return pl.pallas_call(
        functools.partial(_mix_kernel, heads, sides, len(added)),
        out_shape=jax.ShapeDtypeStruct((BLOCK, columns), kind),
        in_specs=[SMEM] + [ANY] * (len(parts) + 2) + [ANY] * len(added),
        out_specs=vmem,
        scratch_shapes=[
            pltpu.VMEM((len(sides), 4, len(heads), BLOCK, HD), jnp.bfloat16),
            pltpu.VMEM((depth, columns), jnp.bfloat16),
            pltpu.VMEM((BLOCK, columns), jnp.float32),
            pltpu.SemaphoreType.DMA((len(sides) * len(heads),)),
            pltpu.SemaphoreType.DMA((4 * len(sides),)),
            pltpu.SemaphoreType.DMA,
        ],
        compiler_params=_params(VMEM_MIB),
        cost_estimate=pl.CostEstimate(
            flops=2 * BLOCK * depth * columns, bytes_accessed=9 * len(heads) * MIB, transcendentals=0
        ),
        name="mix",
    )(place, *parts, w_own, w_other, *added)


def _grad_kernel(count, place, *refs):
    parts, cot = refs[: 4 * count], refs[4 * count]
    sent, kept, left, right, l_sem, r_sem = refs[4 * count + 1 :]
    x, y, c = place[0], place[1], place[2]
    step = pl.program_id(0)

    @pl.when(step == 0)
    def _():
        rows = pltpu.make_async_copy(cot, right, r_sem)
        rows.start()

        def start(turn):
            for n, ref in enumerate(parts):
                head, dx, dy = n // 4, n % 2, n // 2 % 2
                mine = (lax.rem(y + dy, 2) == c).astype(jnp.int32)
                at = 2 * count * mine + count * lax.rem(x + dx, 2) + head
                copy = pltpu.make_async_copy(ref, left.at[at], l_sem.at[at])
                pl.when(mine == turn)(copy.start)

        start(0)
        rows.wait()
        start(1)

    for n in range(count):
        at = count * step + n
        pltpu.make_async_copy(parts[n], left.at[at], l_sem.at[at]).wait()
    rows = jnp.concatenate(
        [
            jnp.concatenate(
                [
                    left[count * step + n, block, tile * HD : (tile + 1) * HD]
                    for block in range(4)
                    for tile in range(BLOCK // HD)
                ],
                axis=1,
            )
            for n in range(count)
        ]
    )
    total = jnp.dot(rows, right[...], preferred_element_type=jnp.float32)

    @pl.when(step < 2)
    def _():
        sent[...] = total.astype(jnp.bfloat16)

    @pl.when(step >= 2)
    def _():
        kept[...] = total


def grad(place, parts, cot):
    count = len(parts) // 4
    rows = count * HD
    tokens, width = cot.shape
    return pl.pallas_call(
        functools.partial(_grad_kernel, count),
        grid=(4,),
        out_shape=(
            jax.ShapeDtypeStruct((2 * rows, width), jnp.bfloat16),
            jax.ShapeDtypeStruct((2 * rows, width), jnp.float32),
        ),
        in_specs=[SMEM] + [ANY] * (len(parts) + 1),
        out_specs=(
            pl.BlockSpec((rows, width), lambda i: (jnp.minimum(i, 1), 0)),
            pl.BlockSpec((rows, width), lambda i: (jnp.maximum(i - 2, 0), 0)),
        ),
        scratch_shapes=[
            pltpu.VMEM((4 * count, 4, BLOCK, HD), jnp.bfloat16),
            pltpu.VMEM((tokens, width), jnp.bfloat16),
            pltpu.SemaphoreType.DMA((4 * count,)),
            pltpu.SemaphoreType.DMA,
        ],
        compiler_params=_params(VMEM_MIB),
        cost_estimate=pl.CostEstimate(
            flops=8 * rows * tokens * width, bytes_accessed=(4 * count + 3) * MIB, transcendentals=0
        ),
        name="grad",
    )(place, *parts, cot)


X_SWAP = [(0, 1), (1, 0), (2, 3), (3, 2)]
Y_SWAP = [(0, 2), (2, 0), (1, 3), (3, 1)]


XY_SWAP = [(0, 3), (3, 0), (1, 2), (2, 1)]
OTHER_CORE = [(0, 1), (1, 0)]


def around(shift):
    return [(i, (i + shift) % 4) for i in range(4)]


def over_row(a, x_first=None):
    if x_first is None:
        return [a] + [lax.ppermute(a, "row", pairs) for pairs in (X_SWAP, Y_SWAP, XY_SWAP)]
    first, second = (X_SWAP, Y_SWAP) if x_first else (Y_SWAP, X_SWAP)
    near = lax.ppermute(a, "row", first)
    far = lax.ppermute(near, "row", second)
    next_to = lax.ppermute(a, "row", second)
    return [a, near, next_to, far] if x_first else [a, next_to, near, far]


def planes_body(queries, keys, values, out_weight, cotangent, block_mask):
    row, c, z = lax.axis_index("row"), lax.axis_index("col"), lax.axis_index("ctx")
    x, y = row % 2, row // 2
    place = jnp.stack([x, y, c, z]).astype(jnp.int32)
    columns = cotangent.shape[1]
    cut = columns // 2

    def exchanged(h, place):
        send, keep = pack(h, place, queries, keys, values)
        got = lax.ppermute(send, "row", X_SWAP)
        return keep, got

    def merged(kept, got):
        return jnp.concatenate([jnp.where(x == 0, kept, got), jnp.where(x == 0, got, kept)])

    def over_ctx(pieces):
        return lax.all_to_all(pieces, "ctx", 0, 0, tiled=True)

    def attended(h, own, beside):
        other = lax.ppermute(own[:, 1:], "col", [(0, 1)])
        out, out_t = attend(place, block_mask, own, other)
        out, out_t, beside = lax.optimization_barrier((out, out_t, beside))
        home = [lax.ppermute(out[s], "ctx", around(s)) for s in range(1, 4)]
        return jnp.stack([out[0]] + home), over_row(out_t, True if h < 2 else None), beside

    first_cot = lax.all_gather(cotangent[:, :cut], "ctx", axis=0, tiled=True)
    pair = exchanged(0, place)
    pair, later = lax.optimization_barrier((pair, place))
    own0 = over_ctx(merged(*pair))
    pairs = [exchanged(h, later) for h in range(1, HALF)]
    w_other = lax.ppermute(out_weight, "col", OTHER_CORE)
    one, two = [merged(*pair) for pair in pairs]
    own0, one, w_other, first_cot = lax.optimization_barrier((own0, one, w_other, first_cot))
    own1 = over_ctx(one)
    home0, grad0, _ = attended(0, own0, ())
    own1, two, home0, grad0 = lax.optimization_barrier((own1, two, home0, grad0))
    own2 = over_ctx(two)
    home1, grad1, _ = attended(1, own1, ())
    mix0 = over_row(home0, False)
    own2, last_half, home1, mix0, grad1 = lax.optimization_barrier(
        (own2, cotangent[:, cut:], home1, mix0, grad1)
    )
    last_cot = lax.all_gather(last_half, "ctx", axis=0, tiled=True)
    mix1 = [home1, lax.ppermute(home1, "row", X_SWAP), lax.ppermute(home1, "row", Y_SWAP)]
    home2, grad2, mix1 = attended(2, own2, mix1)
    mix1.append(lax.ppermute(mix1[2], "row", X_SWAP))
    home2, mix1, grad2[1:3] = lax.optimization_barrier((home2, mix1, grad2[1:3]))
    early = grad(place, grad0 + grad1, first_cot)

    def summed(pairs):
        sent = jnp.concatenate([p[0].reshape(2, -1, p[0].shape[1]) for p in pairs], axis=1)
        kept = jnp.concatenate([p[1].reshape(2, -1, p[1].shape[1]) for p in pairs], axis=1)
        received = lax.ppermute(sent, "col", OTHER_CORE)
        return (kept + received.astype(jnp.float32)).astype(jnp.bfloat16)

    sums = mix(place, (0, 1), mix0 + mix1, out_weight, w_other, None, jnp.float32)
    mix2 = over_row(home2)
    sums, grad2 = lax.optimization_barrier((sums, grad2))
    sums, early, grad2 = lax.optimization_barrier((sums, early, grad2))
    late = grad(place, grad2, first_cot)
    sums = mix(place, (2,), mix2[:2], out_weight, w_other, sums, jnp.float32, (0, 1))
    mix2, last_cot, sums = lax.optimization_barrier((mix2, last_cot, sums))
    last = grad(place, grad0 + grad1 + grad2, last_cot)
    mixed_out = mix(place, (2,), mix2[2:], out_weight, w_other, sums, jnp.bfloat16, (2, 3))
    grad_weight = jnp.concatenate([summed([early, late]), summed([last])], axis=2)
    grad_weight = grad_weight.reshape(-1, columns)
    return (mixed_out, grad_weight)


def solution(mesh):
    in_specs = (
        P(("col", "ctx"), "row"),
        P(("col", "ctx"), "row"),
        P(("col", "ctx"), "row"),
        P("col", "row"),
        P(("col", "ctx"), "row"),
        P(),
    )
    out_specs = (P(("col", "ctx"), "row"), P(("col", "ctx"), "row"))
    four = dict(mesh.shape) == {"row": 4, "col": 2, "ctx": 4}

    def whole(queries, keys, values, out_weight, cotangent, block_mask):
        fits = queries.shape == (8 * BLOCK, 48 * HD)
        body = planes_body if four and fits else gathered_body
        mapped = jax.shard_map(
            body, mesh=mesh, in_specs=in_specs, out_specs=out_specs, check_vma=False
        )
        return mapped(queries, keys, values, out_weight, cotangent, block_mask)

    return whole
```

```python
import functools
import math

import jax
import jax.numpy as jnp
from jax import lax
from jax.experimental import pallas as pl
from jax.experimental.pallas import tpu as pltpu
from jax.sharding import PartitionSpec as P

HD = 128
BLOCK = 512
NEGATIVE_FILL = -1e30
HALF = 3
LOG2E = math.log2(math.e)
MIB = 1 << 20
VMEM_MIB = 56
ANY = pl.BlockSpec(memory_space=pl.ANY)
SMEM = pl.BlockSpec(memory_space=pltpu.SMEM)


def attend_block(carried, query_heads, key_block, value_block, allowed, score_scale):
    run_max, run_sum, weighted = carried
    tok_rows, head_count, head_size = query_heads.shape
    key_heads = key_block.reshape(key_block.shape[0], head_count, head_size)
    value_heads = value_block.reshape(value_block.shape[0], head_count, head_size)
    scores = (
        jnp.einsum("thd,uhd->thu", query_heads, key_heads, preferred_element_type=jnp.float32)
        * score_scale
    )
    scores = jnp.where(allowed[:, None, None], scores, NEGATIVE_FILL)
    new_max = jnp.maximum(run_max, jnp.max(scores, axis=2))
    correction = jnp.exp(run_max - new_max)
    weights = jnp.where(allowed[:, None, None], jnp.exp(scores - new_max[:, :, None]), 0.0)
    new_sum = run_sum * correction + jnp.sum(weights, axis=2)
    product = jnp.einsum(
        "thu,uhd->thd",
        weights.astype(jnp.bfloat16),
        value_heads,
        preferred_element_type=jnp.float32,
    )
    new_weighted = weighted * correction[:, :, None] + product
    return (new_max, new_sum, new_weighted)


def gathered_body(queries, keys, values, out_weight, cotangent, block_mask):
    tok_rows, feature_width = queries.shape
    head_count = feature_width // HD
    query_heads = queries.reshape(tok_rows, head_count, HD)
    score_scale = 1.0 / math.sqrt(HD)
    local_blocks = tok_rows // BLOCK
    first_block = lax.axis_index(("col", "ctx")) * local_blocks
    local_mask = lax.dynamic_slice_in_dim(block_mask, first_block, local_blocks, 0)
    start_state = (
        jnp.full((tok_rows, head_count), NEGATIVE_FILL, jnp.float32),
        jnp.zeros((tok_rows, head_count), jnp.float32),
        jnp.zeros((tok_rows, head_count, HD), jnp.float32),
    )
    key_piece = lax.all_gather(keys, ("col", "ctx"), axis=0, tiled=True)
    value_piece = lax.all_gather(values, ("col", "ctx"), axis=0, tiled=True)
    block_count = key_piece.shape[0] // BLOCK
    key_stack = key_piece.reshape(block_count, BLOCK, feature_width)
    value_stack = value_piece.reshape(block_count, BLOCK, feature_width)
    block_columns = jnp.arange(block_count, dtype=jnp.int32)

    def one_block(state_in, entries):
        key_block, value_block, block_column = entries
        mask_column = lax.dynamic_index_in_dim(local_mask, block_column, 1, keepdims=False)
        allowed = jnp.repeat(mask_column, BLOCK, total_repeat_length=tok_rows) == 1
        updated = attend_block(state_in, query_heads, key_block, value_block, allowed, score_scale)
        return (updated, None)

    state_out, _ = lax.scan(one_block, start_state, (key_stack, value_stack, block_columns))
    run_max, run_sum, weighted = state_out
    attended = (
        (weighted / run_sum[:, :, None]).reshape(tok_rows, feature_width).astype(jnp.bfloat16)
    )
    all_heads = lax.all_gather(attended, "row", axis=1, tiled=True)
    mixed_out = jnp.dot(
        all_heads,
        lax.all_gather(out_weight, "col", axis=0, tiled=True),
        preferred_element_type=jnp.float32,
    )
    grad_weight = lax.psum_scatter(
        lax.dot_general(
            all_heads, cotangent, (((0,), (0,)), ((), ())), preferred_element_type=jnp.float32
        ),
        ("col", "ctx"),
        scatter_dimension=0,
        tiled=True,
    )
    return (mixed_out.astype(jnp.bfloat16), grad_weight.astype(jnp.bfloat16))


def _params(mib):
    return pltpu.CompilerParams(vmem_limit_bytes=mib * MIB)


def _pack_kernel(place, *refs):
    columns, (send, keep) = refs[:6], refs[6:]
    for out, first in ((send, 0), (keep, 3)):
        out[0, 0] = columns[first][...]
        out[0, 1] = columns[first + 1][...]
        for n in range(BLOCK // HD):
            tile = slice(n * HD, (n + 1) * HD)
            out[0, 2, tile] = columns[first + 2][tile, :].T


def pack(head, place, q, k, v):
    shape = jax.ShapeDtypeStruct((2, 3, BLOCK, HD), jnp.bfloat16)

    def column(kept):
        def at(low, place_ref):
            side = place_ref[0] if kept else 1 - place_ref[0]
            return (0, 6 * low + 3 * side + head)

        return pl.BlockSpec((BLOCK, HD), at)

    out = pl.BlockSpec((1, 3, BLOCK, HD), lambda low, place_ref: (low, 0, 0, 0))
    return pl.pallas_call(
        _pack_kernel,
        grid_spec=pltpu.PrefetchScalarGridSpec(
            num_scalar_prefetch=1,
            grid=(2,),
            in_specs=[column(False)] * 3 + [column(True)] * 3,
            out_specs=(out, out),
        ),
        out_shape=(shape, shape),
        cost_estimate=pl.CostEstimate(flops=0, bytes_accessed=3 * MIB, transcendentals=0),
        name="pack",
    )(place, q, k, v, q, k, v)


def _attend_kernel(place, mask, *refs):
    own, other = refs[0], refs[1]
    out, out_t = refs[2:4]
    q_s, k_s, vt_s, sa_s, sb_s, m_s, l_s, acc_s, rows_s, cols_s, sems, other_sems = refs[4:]
    c, z = place[2], place[3]
    first = 4 * c
    copies = []
    others = []
    for s in range(4):
        b = s
        copies.append(pltpu.make_async_copy(own.at[s, 0], q_s.at[b], sems.at[2 * s]))
        copies.append(pltpu.make_async_copy(own.at[s, 1], k_s.at[first + b], sems.at[2 * s + 1]))
        for n in range(4):
            tile = pl.ds(n * HD, HD)
            copies.append(
                pltpu.make_async_copy(
                    own.at[s, 2, tile], vt_s.at[first + b, :, tile], sems.at[8 + 4 * s + n]
                )
            )
        others.append(pltpu.make_async_copy(other.at[s, 0], k_s.at[b], other_sems.at[s]))
        for n in range(4):
            tile = pl.ds(n * HD, HD)
            others.append(
                pltpu.make_async_copy(
                    other.at[s, 1, tile], vt_s.at[b, :, tile], other_sems.at[4 + 4 * s + n]
                )
            )
    for copy in copies:
        copy.start()

    @pl.when(c == 1)
    def _():
        for copy in others:
            copy.start()

    def listed(n, count):
        i, j = n // 8, lax.rem(n, 8)
        rows_s[count] = i
        cols_s[count] = j
        taken = (j <= first + i) & (mask[first + i, j] == 1)
        return count + taken.astype(jnp.int32)

    count = lax.fori_loop(0, 32, listed, 0)
    for extra in range(3):
        rows_s[count + extra] = 3
        cols_s[count + extra] = first + 3

    l_s[...] = jnp.zeros_like(l_s)
    acc_s[...] = jnp.zeros_like(acc_s)
    for copy in copies:
        copy.wait()

    @pl.when(c == 1)
    def _():
        for copy in others:
            copy.wait()

    scale = LOG2E / math.sqrt(HD)

    def scores(t, ref):
        ref[...] = lax.dot_general(
            k_s[cols_s[t]], q_s[rows_s[t]], (((1,), (1,)), ((), ())), preferred_element_type=jnp.float32
        )

    def step(t, now, later):
        i, j = rows_s[t], cols_s[t]
        fresh = (t == 0) | (rows_s[jnp.maximum(t - 1, 0)] != i)
        scores(t + 1, later)
        old = jnp.where(fresh, NEGATIVE_FILL, m_s[...])
        s = now[...]
        m = jnp.maximum(old, jnp.max(s, axis=0, keepdims=True) * scale)
        p = jnp.exp2(s * scale - m)
        fix = jnp.exp2(old - m)
        m_s[...] = m
        l = l_s[...] * fix + jnp.sum(p, axis=0, keepdims=True)
        l_s[...] = l
        acc = acc_s[...] * fix + jnp.dot(vt_s[j], p.astype(jnp.bfloat16), preferred_element_type=jnp.float32)
        acc_s[...] = acc

        @pl.when((j == first + i) & (t < count))
        def _():
            done = acc_s[...] / l_s[...]
            for n in range(BLOCK // HD):
                tile = slice(n * HD, (n + 1) * HD)
                out_t[i, tile] = done[:, tile].astype(jnp.bfloat16)
            out[lax.rem(i - z + 4, 4)] = done.T.astype(jnp.bfloat16)

    scores(0, sa_s)

    def two(u, _):
        step(2 * u, sa_s, sb_s)
        step(2 * u + 1, sb_s, sa_s)
        return 0

    lax.fori_loop(0, (count + 1) // 2, two, 0)


def attend(place, mask, own, other):
    vmem = pl.BlockSpec(memory_space=pltpu.VMEM)
    return pl.pallas_call(
        _attend_kernel,
        out_shape=(
            jax.ShapeDtypeStruct((4, BLOCK, HD), jnp.bfloat16),
            jax.ShapeDtypeStruct((4, BLOCK, HD), jnp.bfloat16),
        ),
        in_specs=[SMEM, SMEM, ANY, ANY],
        out_specs=(vmem, vmem),
        scratch_shapes=[
            pltpu.VMEM((4, BLOCK, HD), jnp.bfloat16),
            pltpu.VMEM((8, BLOCK, HD), jnp.bfloat16),
            pltpu.VMEM((8, HD, BLOCK), jnp.bfloat16),
            pltpu.VMEM((BLOCK, BLOCK), jnp.float32),
            pltpu.VMEM((BLOCK, BLOCK), jnp.float32),
            pltpu.VMEM((1, BLOCK), jnp.float32),
            pltpu.VMEM((1, BLOCK), jnp.float32),
            pltpu.VMEM((HD, BLOCK), jnp.float32),
            pltpu.SMEM((40,), jnp.int32),
            pltpu.SMEM((40,), jnp.int32),
            pltpu.SemaphoreType.DMA((24,)),
            pltpu.SemaphoreType.DMA((20,)),
        ],
        compiler_params=_params(VMEM_MIB),
        cost_estimate=pl.CostEstimate(
            flops=20 * 4 * BLOCK * BLOCK * HD,
            bytes_accessed=4 * MIB,
            transcendentals=20 * BLOCK * BLOCK,
        ),
        name="attend",
    )(place, mask, own, other)


def _mix_kernel(heads, sides, added, place, *refs):
    count = len(sides) * len(heads)
    parts, (w_own, w_other) = refs[:count], refs[count : count + 2]
    sums = refs[count + 2] if added else None
    out = refs[count + 2 + added]
    a_s, w_s, sum_s, a_sem, w_sem, s_sem = refs[count + 3 + added :]
    x, y, c, z = place[0], place[1], place[2], place[3]
    depth = len(heads) * HD

    def attended(n, side):
        return pltpu.make_async_copy(
            parts[len(sides) * n + side], a_s.at[side, :, n], a_sem.at[len(sides) * n + side]
        )

    def weight(side, block, ref):
        xx = lax.rem(x + sides[side] % 2, 2)
        from_z = lax.rem(z - block + 4, 4)
        at = pl.multiple_of((6 * from_z + 3 * xx + heads[0]) * HD, HD)
        return pltpu.make_async_copy(
            ref.at[pl.ds(at, depth)],
            w_s.at[pl.ds((4 * side + block) * depth, depth)],
            w_sem.at[4 * side + block],
        )

    def fetch(side):
        yy = lax.rem(y + sides[side] // 2, 2)
        for n in range(len(heads)):
            attended(n, side).start()
        for block in range(4):
            pl.when(yy == c)(weight(side, block, w_own).start)
            pl.when(yy != c)(weight(side, block, w_other).start)

    if added:
        known = pltpu.make_async_copy(sums, sum_s, s_sem)
        known.start()
    fetch(0)
    fetch(1)
    width = 512
    piece = 8 * depth
    halves = len(sides) // 2
    for half in range(halves):
        for side in (2 * half, 2 * half + 1):
            if half < halves - 1:
                fetch(side + 2)
            for n in range(len(heads)):
                attended(n, side).wait()
            for block in range(4):
                weight(side, block, w_own).wait()
        if half == 0 and added:
            known.wait()

        def tile(t, _, half=half):
            cut = pl.ds(pl.multiple_of(t * width, width), width)
            rows = jnp.concatenate(
                [
                    a_s[side, block, n]
                    for side in (2 * half, 2 * half + 1)
                    for block in range(4)
                    for n in range(len(heads))
                ],
                axis=1,
            )
            term = jnp.dot(
                rows, w_s[half * piece : (half + 1) * piece, cut], preferred_element_type=jnp.float32
            )
            if half > 0 or added:
                term += sum_s[:, cut]
            if half < halves - 1:
                sum_s[:, cut] = term
            else:
                out[:, cut] = term.astype(out.dtype)
            return 0

        lax.fori_loop(0, out.shape[1] // width, tile, 0)


def mix(place, heads, parts, w_own, w_other, sums, kind, sides=(0, 1, 2, 3)):
    columns = w_own.shape[1]
    depth = 4 * len(sides) * len(heads) * HD
    vmem = pl.BlockSpec(memory_space=pltpu.VMEM)
    added = [] if sums is None else [sums]
    return pl.pallas_call(
        functools.partial(_mix_kernel, heads, sides, len(added)),
        out_shape=jax.ShapeDtypeStruct((BLOCK, columns), kind),
        in_specs=[SMEM] + [ANY] * (len(parts) + 2) + [ANY] * len(added),
        out_specs=vmem,
        scratch_shapes=[
            pltpu.VMEM((len(sides), 4, len(heads), BLOCK, HD), jnp.bfloat16),
            pltpu.VMEM((depth, columns), jnp.bfloat16),
            pltpu.VMEM((BLOCK, columns), jnp.float32),
            pltpu.SemaphoreType.DMA((len(sides) * len(heads),)),
            pltpu.SemaphoreType.DMA((4 * len(sides),)),
            pltpu.SemaphoreType.DMA,
        ],
        compiler_params=_params(VMEM_MIB),
        cost_estimate=pl.CostEstimate(
            flops=2 * BLOCK * depth * columns, bytes_accessed=9 * len(heads) * MIB, transcendentals=0
        ),
        name="mix",
    )(place, *parts, w_own, w_other, *added)


def _grad_kernel(count, place, *refs):
    parts, cot = refs[: 4 * count], refs[4 * count]
    sent, kept, left, right, l_sem, r_sem = refs[4 * count + 1 :]
    x, y, c = place[0], place[1], place[2]
    step = pl.program_id(0)

    @pl.when(step == 0)
    def _():
        rows = pltpu.make_async_copy(cot, right, r_sem)
        rows.start()

        def start(turn):
            for n, ref in enumerate(parts):
                head, dx, dy = n // 4, n % 2, n // 2 % 2
                mine = (lax.rem(y + dy, 2) == c).astype(jnp.int32)
                at = 2 * count * mine + count * lax.rem(x + dx, 2) + head
                copy = pltpu.make_async_copy(ref, left.at[at], l_sem.at[at])
                pl.when(mine == turn)(copy.start)

        start(0)
        rows.wait()
        start(1)

    for n in range(count):
        at = count * step + n
        pltpu.make_async_copy(parts[n], left.at[at], l_sem.at[at]).wait()
    rows = jnp.concatenate(
        [
            jnp.concatenate(
                [
                    left[count * step + n, block, tile * HD : (tile + 1) * HD]
                    for block in range(4)
                    for tile in range(BLOCK // HD)
                ],
                axis=1,
            )
            for n in range(count)
        ]
    )
    total = jnp.dot(rows, right[...], preferred_element_type=jnp.float32)

    @pl.when(step < 2)
    def _():
        sent[...] = total.astype(jnp.bfloat16)

    @pl.when(step >= 2)
    def _():
        kept[...] = total


def grad(place, parts, cot):
    count = len(parts) // 4
    rows = count * HD
    tokens, width = cot.shape
    return pl.pallas_call(
        functools.partial(_grad_kernel, count),
        grid=(4,),
        out_shape=(
            jax.ShapeDtypeStruct((2 * rows, width), jnp.bfloat16),
            jax.ShapeDtypeStruct((2 * rows, width), jnp.float32),
        ),
        in_specs=[SMEM] + [ANY] * (len(parts) + 1),
        out_specs=(
            pl.BlockSpec((rows, width), lambda i: (jnp.minimum(i, 1), 0)),
            pl.BlockSpec((rows, width), lambda i: (jnp.maximum(i - 2, 0), 0)),
        ),
        scratch_shapes=[
            pltpu.VMEM((4 * count, 4, BLOCK, HD), jnp.bfloat16),
            pltpu.VMEM((tokens, width), jnp.bfloat16),
            pltpu.SemaphoreType.DMA((4 * count,)),
            pltpu.SemaphoreType.DMA,
        ],
        compiler_params=_params(VMEM_MIB),
        cost_estimate=pl.CostEstimate(
            flops=8 * rows * tokens * width, bytes_accessed=(4 * count + 3) * MIB, transcendentals=0
        ),
        name="grad",
    )(place, *parts, cot)


X_SWAP = [(0, 1), (1, 0), (2, 3), (3, 2)]
Y_SWAP = [(0, 2), (2, 0), (1, 3), (3, 1)]


XY_SWAP = [(0, 3), (3, 0), (1, 2), (2, 1)]
OTHER_CORE = [(0, 1), (1, 0)]


def around(shift):
    return [(i, (i + shift) % 4) for i in range(4)]


def over_row(a, x_first=None):
    if x_first is None:
        return [a] + [lax.ppermute(a, "row", pairs) for pairs in (X_SWAP, Y_SWAP, XY_SWAP)]
    first, second = (X_SWAP, Y_SWAP) if x_first else (Y_SWAP, X_SWAP)
    near = lax.ppermute(a, "row", first)
    far = lax.ppermute(near, "row", second)
    next_to = lax.ppermute(a, "row", second)
    return [a, near, next_to, far] if x_first else [a, next_to, near, far]


def planes_body(queries, keys, values, out_weight, cotangent, block_mask):
    row, c, z = lax.axis_index("row"), lax.axis_index("col"), lax.axis_index("ctx")
    x, y = row % 2, row // 2
    place = jnp.stack([x, y, c, z]).astype(jnp.int32)
    columns = cotangent.shape[1]
    cut = columns // 2

    def exchanged(h, place):
        send, keep = pack(h, place, queries, keys, values)
        got = lax.ppermute(send, "row", X_SWAP)
        return keep, got

    def merged(kept, got):
        return jnp.concatenate([jnp.where(x == 0, kept, got), jnp.where(x == 0, got, kept)])

    def over_ctx(pieces):
        return lax.all_to_all(pieces, "ctx", 0, 0, tiled=True)

    def attended(h, own, beside):
        other = lax.ppermute(own[:, 1:], "col", [(0, 1)])
        out, out_t = attend(place, block_mask, own, other)
        out, out_t, beside = lax.optimization_barrier((out, out_t, beside))
        home = [lax.ppermute(out[s], "ctx", around(s)) for s in range(1, 4)]
        return jnp.stack([out[0]] + home), over_row(out_t, True if h < 2 else None), beside

    first_cot = lax.all_gather(cotangent[:, :cut], "ctx", axis=0, tiled=True)
    pair = exchanged(0, place)
    pair, later = lax.optimization_barrier((pair, place))
    own0 = over_ctx(merged(*pair))
    pairs = [exchanged(h, later) for h in range(1, HALF)]
    w_other = lax.ppermute(out_weight, "col", OTHER_CORE)
    one, two = [merged(*pair) for pair in pairs]
    own0, one, w_other, first_cot = lax.optimization_barrier((own0, one, w_other, first_cot))
    own1 = over_ctx(one)
    home0, grad0, _ = attended(0, own0, ())
    own1, two, home0, grad0 = lax.optimization_barrier((own1, two, home0, grad0))
    own2 = over_ctx(two)
    home1, grad1, _ = attended(1, own1, ())
    mix0 = over_row(home0, False)
    own2, last_half, home1, mix0, grad1 = lax.optimization_barrier(
        (own2, cotangent[:, cut:], home1, mix0, grad1)
    )
    last_cot = lax.all_gather(last_half, "ctx", axis=0, tiled=True)
    mix1 = [home1, lax.ppermute(home1, "row", X_SWAP), lax.ppermute(home1, "row", Y_SWAP)]
    home2, grad2, mix1 = attended(2, own2, mix1)
    mix1.append(lax.ppermute(mix1[2], "row", X_SWAP))
    home2, mix1, grad2[1:3] = lax.optimization_barrier((home2, mix1, grad2[1:3]))
    early = grad(place, grad0 + grad1, first_cot)

    def summed(pairs):
        sent = jnp.concatenate([p[0].reshape(2, -1, p[0].shape[1]) for p in pairs], axis=1)
        kept = jnp.concatenate([p[1].reshape(2, -1, p[1].shape[1]) for p in pairs], axis=1)
        received = lax.ppermute(sent, "col", OTHER_CORE)
        return (kept + received.astype(jnp.float32)).astype(jnp.bfloat16)

    sums = mix(place, (0, 1), mix0 + mix1, out_weight, w_other, None, jnp.float32)
    mix2 = over_row(home2)
    sums, grad2 = lax.optimization_barrier((sums, grad2))
    sums, early, grad2 = lax.optimization_barrier((sums, early, grad2))
    late = grad(place, grad2, first_cot)
    sums = mix(place, (2,), mix2[:2], out_weight, w_other, sums, jnp.float32, (0, 1))
    first = summed([early, late])
    mix2, last_cot, sums, first = lax.optimization_barrier((mix2, last_cot, sums, first))
    last = grad(place, grad0 + grad1 + grad2, last_cot)
    mixed_out = mix(place, (2,), mix2[2:], out_weight, w_other, sums, jnp.bfloat16, (2, 3))
    grad_weight = jnp.concatenate([first, summed([last])], axis=2)
    grad_weight = grad_weight.reshape(-1, columns)
    return (mixed_out, grad_weight)


def solution(mesh):
    in_specs = (
        P(("col", "ctx"), "row"),
        P(("col", "ctx"), "row"),
        P(("col", "ctx"), "row"),
        P("col", "row"),
        P(("col", "ctx"), "row"),
        P(),
    )
    out_specs = (P(("col", "ctx"), "row"), P(("col", "ctx"), "row"))
    four = dict(mesh.shape) == {"row": 4, "col": 2, "ctx": 4}

    def whole(queries, keys, values, out_weight, cotangent, block_mask):
        fits = queries.shape == (8 * BLOCK, 48 * HD)
        body = planes_body if four and fits else gathered_body
        mapped = jax.shard_map(
            body, mesh=mesh, in_specs=in_specs, out_specs=out_specs, check_vma=False
        )
        return mapped(queries, keys, values, out_weight, cotangent, block_mask)

    return whole
```
